128 devices in a mesh: band: 32 (over z, y, x_hi), pair: 4 (over x_lo, core).
Axes of the slice: x: 4 (x_hi: 2, x_lo: 2; x = x_hi * 2 + x_lo), y: 4, z: 4, core: 2. Of those that a mesh axis runs over, the one named last changes fastest.
Arguments:
- orbitals: float32 [32, 64, 4096], P('band'), may hold values from -3 to 3
- pair_keep: int32 [32, 32], replicated, may hold values from 0 to 1, as said below
Outputs:
- exchange: float32 [32, 64, 4096], P('band', 'pair')
The draws below stay inside these ranges and needn't reach their ends.
Inputs may be any that keep to these rules, and one draw needn't show every extreme that they name: pair_keep is symmetric with ones on its diagonal; orbital i belongs to block i.
All inputs are finite; a program needn't handle non-finite values.
Results may differ from the reference program's by a relative error of at most 0.00018.
Values sent between devices are 32-bit elements; how exact they have to be, the bound alone decides.
A program may use at most 128 MiB of HBM per device.

```python
import math
import jax
import jax.numpy as jnp
from jax import lax

NX = 64
NY = 64
NZ = 64
ORB_DEV = 1
NORB = 32
NYZ = 4096
N_BAND = 32


def draw_pair_keep(key, part):
    key = jax.random.fold_in(key, 7)
    random_draws = jax.random.randint(key, (NORB, NORB), 0, 1000, dtype=jnp.int32)
    orbital_ids = jnp.arange(NORB, dtype=jnp.int32)
    block_ids = orbital_ids // ORB_DEV
    cycle_gap = (block_ids[None, :] - block_ids[:, None]) % N_BAND
    distance = jnp.minimum(cycle_gap, N_BAND - cycle_gap)
    threshold = 1000 - 700 * distance // (N_BAND // 2)
    upper_mask = orbital_ids[None, :] >= orbital_ids[:, None]
    symmetric = jnp.where(upper_mask, random_draws, random_draws.T)
    return (symmetric < threshold).astype(jnp.int32)


def level_of(own_key, shape, cuts, least, largest):
    level, own = 1.0, jax.random.fold_in(own_key, 6)
    for position, shards_of in cuts:
        heights = jnp.exp(jax.random.uniform(jax.random.fold_in(own, position), (shards_of,), jnp.float32, least / len(cuts), largest / len(cuts)))
        level = level * jnp.repeat(heights, shape[position] // shards_of).reshape([-1 if axis == position else 1 for axis in range(len(shape))])
    return level


def normal_values(own_key, extent, deviation, most, shards=(), held_as=jnp.bfloat16):
    drawn = jax.random.normal(own_key, extent, jnp.float32) * deviation
    if len(shards) > 0:
        drawn = level_of(own_key, extent, shards, -0.22, 0.18) * drawn
    return jnp.clip(drawn, min=-most, max=most).astype(held_as)


def setup_inputs(seed: int = 0) -> dict:
    key_of = jax.random.split(jax.random.key(seed), 3)
    return {
        "orbitals": normal_values(key_of[0], (NORB, NX, NYZ), 0.5, 3.0, ((0, 32),), jnp.float32),
        "pair_keep": draw_pair_keep(jax.random.fold_in(key_of[2], 71), 0),
    }


CELL_LENGTH = 46.92
SCREEN_OMEGA = 0.11


def wave_numbers(length):
    counter = jnp.arange(length, dtype=jnp.int32)
    return jnp.minimum(counter, length - counter).astype(jnp.float32) * (2.0 * math.pi / CELL_LENGTH)


def screened_kernel():
    wave_x = wave_numbers(NX)
    wave_y = wave_numbers(NY)
    wave_z = wave_numbers(NZ)
    square = wave_x[:, None, None] ** 2 + wave_y[None, :, None] ** 2 + wave_z[None, None, :] ** 2
    guarded = jnp.where(square > 0.0, square, 1.0)
    screened = (4.0 * math.pi / guarded) * (-jnp.expm1(-guarded / (4.0 * SCREEN_OMEGA * SCREEN_OMEGA)))
    return jnp.where(square > 0.0, screened, 0.0)


def reference(orbitals, pair_keep):
    orbital_grid = orbitals.reshape(NORB, NX, NY, NZ)
    kernel = -screened_kernel()[:, :, : NZ // 2 + 1]
    orbital_ids = jnp.arange(NORB, dtype=jnp.int32)
    upper_mask = (orbital_ids[None, :] >= orbital_ids[:, None]).astype(orbitals.dtype)
    weights = pair_keep.astype(orbitals.dtype) * upper_mask

    def add_row(orbital_index, summed):
        own_orbital = lax.dynamic_slice_in_dim(orbital_grid, orbital_index, 1, 0)
        spectrum = jnp.fft.rfftn(own_orbital * orbital_grid, axes=(1, 2, 3))
        potential = jnp.fft.irfftn(spectrum * kernel, s=(NX, NY, NZ), axes=(1, 2, 3)).astype(orbitals.dtype)
        row_weight = lax.dynamic_slice_in_dim(weights, orbital_index, 1, 0)[0]
        strict = row_weight * (orbital_ids != orbital_index).astype(orbitals.dtype)
        own_term = jnp.sum(row_weight[:, None, None, None] * potential * orbital_grid, axis=0, keepdims=True)
        updated = lax.dynamic_slice_in_dim(summed, orbital_index, 1, 0) + own_term
        summed = lax.dynamic_update_slice_in_dim(summed, updated, orbital_index, 0)
        return summed + strict[:, None, None, None] * potential * own_orbital

    summed = lax.fori_loop(0, NORB, add_row, jnp.zeros_like(orbital_grid))
    return summed.reshape(NORB, NX, NY * NZ)
```

```python
import functools
import math

import jax
import jax.numpy as jnp
import ml_dtypes
import numpy as np
from jax import lax
from jax.experimental import pallas as pl
from jax.experimental.pallas import tpu as pltpu
from jax.sharding import PartitionSpec as P

NX = NY = NZ = 64
NYZ = NY * NZ
CELL_LENGTH = 46.92
SCREEN_OMEGA = 0.11
BF16 = jnp.bfloat16
F32 = jnp.float32
MESH = pl.DeviceIdType.MESH

ELEMENTS = [[((0, 1, 0), (0, 1, 0), None), ((0, 0, 1), (0, 0, 1), None), ((1, 3, 0), (1, 3, 0), None), ((2, 0, 1), (2, 0, 1), None), ((3, 0, 0), (3, 0, 0), None)], [((1, 0, 0), (1, 0, 0), None), ((3, 0, 0), (3, 2, 0), 0), ((1, 0, 1), (1, 0, 1), None), ((0, 2, 0), (0, 2, 0), None), ((0, 0, 1), (0, 0, 1), None)]]
EARLY = [4, 4]
EARLY_BACK = [[1, 3], [1, 2]]
LATE_BACK = [[0, 2, 4], [0, 3, 4]]
PAIRS = [[[[(3, 4, 3, 4, None, 0), (2, 3, 2, 3, None, 0)], [(0, 3, 0, 3, None, 0), (3, 5, 3, 5, None, 0)]], [[(2, 1, 2, 1, None, 0), (4, 1, 4, 1, None, 0)], [(0, 1, 0, 1, None, 0), (5, 1, 5, 1, None, 0)]]], [[[(1, 2, 1, 2, 0, 0), (3, 2, 3, 2, 0, 0)], [(0, 1, 0, 1, None, 0), (4, 1, 4, 1, None, 0)]], [[(0, 3, 0, 3, None, 0), (4, 3, 4, 3, None, 0)], [(4, 0, 4, 5, 1, 0), (0, 5, 0, 5, None, 1)]]]]
K = max(len(ELEMENTS[0]), len(ELEMENTS[1]))
JC = 8
YC = 2 * JC


def cas_matrix():
    counter = np.arange(64)
    angles = 2.0 * math.pi * (np.outer(counter, counter) % 64) / 64
    return np.cos(angles) + np.sin(angles)


def split_constant(matrix):
    high = matrix.astype(ml_dtypes.bfloat16)
    low = (matrix - high.astype(np.float64)).astype(ml_dtypes.bfloat16)
    return high, low


def lane_matrix():
    high, low = split_constant(np.kron(np.eye(2), cas_matrix()))
    row = np.concatenate([high, low], axis=1)
    return np.concatenate([row, row], axis=0)


def sublane_matrix():
    high, low = split_constant(cas_matrix())
    return np.concatenate([np.concatenate([high, high], 1), np.concatenate([low, low], 1)], 0)


def screened_table():
    counter = np.arange(64)
    wave = np.minimum(counter, 64 - counter) * (2.0 * math.pi / CELL_LENGTH)
    square = wave[:, None, None] ** 2 + wave[None, :, None] ** 2 + wave[None, None, :] ** 2
    guarded = np.where(square > 0.0, square, 1.0)
    screened = 4.0 * math.pi / guarded * -np.expm1(-guarded / (4.0 * SCREEN_OMEGA**2))
    table = np.where(square > 0.0, screened, 0.0) * (-1.0 / (NX * NY * NZ))
    return np.concatenate([table, table], axis=2).astype(np.float32)


def dot(a, b):
    return jnp.dot(a, b, preferred_element_type=F32)


def halves(v):
    high = v.astype(BF16)
    low = (v - high.astype(F32)).astype(BF16)
    return high, low


def along_lanes(v, weights):
    out = dot(jnp.concatenate(halves(v), axis=1), weights)
    return out[:, :128] + out[:, 128:]


def along_rows(v, weights):
    out = dot(weights, jnp.concatenate(halves(v), axis=0))
    return out[:64] + out[64:]


def rows_to_lanes(v, count):
    return jnp.concatenate([v[64 * i : 64 * i + 64] for i in range(count)], axis=1)


def lanes_to_rows(v, count):
    return jnp.concatenate([v[:, 128 * i : 128 * i + 128] for i in range(count)], axis=0)


class Place:
    def __init__(self):
        band = lax.axis_index("band")
        pair = lax.axis_index("pair")
        self.z, self.y, self.h = band // 8, (band // 2) % 4, band % 2
        self.l, self.c = pair // 2, pair % 2
        self.band = band

    def shifted(self, u, sign):
        z = (self.z + 4 + sign * u[0]) % 4
        y = (self.y + 4 + sign * u[1]) % 4
        h = (self.h + u[2]) % 2
        return z, y, h

    def band_at(self, u, sign):
        z, y, h = self.shifted(u, sign)
        return (z * 4 + y) * 2 + h

    def phase_at(self, phase, u, sign):
        z, y, _ = self.shifted(u, sign)
        return (z // 2) if phase == 0 else (y // 2)


def variants(element):
    first, second, phase = element
    if phase is None:
        return [(first, None, 0)]
    return [(first, phase, 0), (second, phase, 1)]


def hosts(place):
    found = []
    for host_l in (0, 1):
        for e, element in enumerate(ELEMENTS[host_l]):
            for v, (u, phase, value) in enumerate(variants(element)):
                here = host_l if u[2] == 0 else 1 - host_l
                condition = place.l == here
                if phase is not None:
                    condition = condition & (place.phase_at(phase, u, -1) == value)
                found.append((host_l, e, u, condition))
    return found


def wants(place):
    found = []
    for host_l in (0, 1):
        for e, element in enumerate(ELEMENTS[host_l]):
            for v, (u, phase, value) in enumerate(variants(element)):
                condition = place.l == host_l
                if phase is not None:
                    condition = condition & (place.phase_at(phase, (0, 0, 0), 1) == value)
                there = host_l if u[2] == 0 else 1 - host_l
                found.append((host_l, e, u, there, condition))
    return found


def kernel(orb_ref, keep_ref, wz_ref, wr_ref, table_hbm, out_ref,
           slots, acc, xbuf, rbuf, fbuf, spect, table,
           local_sem, d_send, d_recv, f_send, f_recv, x_send, x_recv, r_send, r_recv, s_sem):
    at = Place()
    l, c = at.l, at.c
    sibling = (at.band, 2 * l + 1 - c)
    twin = (at.band, 2 * (1 - l) + c)

    def pick(values):
        out = 0
        for (pl_, pc_), value in values.items():
            if value != 0:
                out = out + value * ((l == pl_) & (c == pc_)).astype(jnp.int32)
        return out

    own_copy = pltpu.make_async_copy(orb_ref, slots.at[0], local_sem.at[0])
    own_copy.start()
    table_copy = pltpu.make_async_copy(table_hbm, table, local_sem.at[1])
    table_copy.start()

    barrier = pltpu.get_barrier_semaphore()
    peers = 2
    pl.semaphore_signal(barrier, inc=1, device_id=sibling, device_id_type=MESH)
    pl.semaphore_signal(barrier, inc=1, device_id=twin, device_id_type=MESH)
    host_list, want_list = hosts(at), wants(at)
    for host_l, e, u, condition in host_list:
        peers = peers + condition.astype(jnp.int32)
        device = (at.band_at(u, -1), 2 * host_l + c)

        @pl.when(condition)
        def _():
            pl.semaphore_signal(barrier, inc=1, device_id=device, device_id_type=MESH)

    for host_l, e, u, there, condition in want_list:
        peers = peers + condition.astype(jnp.int32)
        device = (at.band_at(u, 1), 2 * there + c)

        @pl.when(condition)
        def _():
            pl.semaphore_signal(barrier, inc=1, device_id=device, device_id_type=MESH)

    for e in range(1, K + 1):
        acc[e] = jnp.zeros(acc.shape[1:], F32)
    own_copy.wait()
    pl.semaphore_wait(barrier, peers)

    my_rows = pl.ds(pl.multiple_of(32 * c, 32), 32)

    def orbital_out(host_l, e, u):
        return pltpu.make_async_remote_copy(
            src_ref=slots.at[0, my_rows], dst_ref=slots.at[e + 1, my_rows],
            send_sem=d_send.at[host_l * K + e], recv_sem=d_recv.at[e],
            device_id=(at.band_at(u, -1), 2 * host_l + c), device_id_type=MESH)

    for host_l, e, u, condition in sorted(host_list, key=lambda t: t[1]):

        @pl.when(condition)
        def _():
            orbital_out(host_l, e, u).start()

    def forward(e):
        return pltpu.make_async_remote_copy(
            src_ref=slots.at[e + 1, my_rows], dst_ref=slots.at[e + 1, my_rows],
            send_sem=f_send.at[e], recv_sem=f_recv.at[e], device_id=sibling, device_id_type=MESH)

    def for_elements(first, body):
        for host_l in (0, 1):
            chosen = [e for e in range(len(ELEMENTS[host_l])) if (e < EARLY[host_l]) == first]

            @pl.when(l == host_l)
            def _():
                for e in chosen:
                    body(e)

    def pass_on(e):
        orbital_out(0, e, (0, 0, 0)).wait_recv()
        forward(e).start()

    def pass_done(e):
        forward(e).wait()

    low_lanes = lax.broadcasted_iota(jnp.int32, (64, 128), 1) < 64

    def lanes_of(i):
        return pl.ds(pl.multiple_of(i * (128 * JC), 128 * JC), 128 * JC)

    def transform(pairs, update, between):
        wz, wr = wz_ref[...], wr_ref[...]
        (p0, q0), (p1, q1) = pairs

        def first(i, carry):
            lanes = lanes_of(i)
            d0 = slots[p0, :, lanes] * slots[q0, :, lanes]
            d1 = slots[p1, :, lanes] * slots[q1, :, lanes]
            tiles = []
            for j in range(JC):
                t0, t1 = d0[:, 128 * j : 128 * j + 128], d1[:, 128 * j : 128 * j + 128]
                tiles.append(jnp.where(low_lanes, t0, pltpu.roll(t1, 64, 1)))
                tiles.append(jnp.where(low_lanes, pltpu.roll(t0, 64, 1), t1))
            v = along_lanes(jnp.concatenate(tiles, axis=0), wz)
            v = along_rows(rows_to_lanes(v, YC), wr)
            spect[pl.ds(pl.multiple_of(i * (64 * YC), 64 * YC), 64 * YC), :] = lanes_to_rows(v, YC)
            return carry

        def second(i, carry):
            rows = [pl.ds(i * YC + k, 64, stride=64) for k in range(YC)]
            v = along_rows(jnp.concatenate([spect[r, :] for r in rows], axis=1), wr)
            scale = jnp.concatenate([table[i * YC + k] for k in range(YC)], axis=1)
            v = along_rows(v * scale, wr)
            for k in range(YC):
                spect[rows[k], :] = v[:, 128 * k : 128 * k + 128]
            return carry

        def third(i, carry):
            v = spect[pl.ds(pl.multiple_of(i * (64 * YC), 64 * YC), 64 * YC), :]
            v = along_rows(rows_to_lanes(v, YC), wr)
            v = along_lanes(lanes_to_rows(v, YC), wz)
            v0, v1 = [], []
            for j in range(JC):
                even, odd = v[128 * j : 128 * j + 64], v[128 * j + 64 : 128 * j + 128]
                v0.append(jnp.where(low_lanes, even, pltpu.roll(odd, 64, 1)))
                v1.append(jnp.where(low_lanes, pltpu.roll(even, 64, 1), odd))
            update(lanes_of(i), jnp.concatenate(v0, axis=1), jnp.concatenate(v1, axis=1))
            return carry

        lax.fori_loop(0, 64 // YC, first, 0)
        lax.fori_loop(0, 64 // YC, second, 0)
        between()
        lax.fori_loop(0, 64 // YC, third, 0)

    def keep_at(i, j):
        return keep_ref[i, j].astype(F32)

    self_keep = keep_at(at.band, at.band)

    def self_update(lanes, v0, v1):
        orbital = slots[0, :, lanes]
        for s in range(4):
            rows = slice(16 * s, 16 * s + 16)
            mine = self_keep * (2 * l + c == s).astype(F32)
            acc[0, s % 2, s // 2, :, lanes] = (mine * v0[rows]) * orbital[rows]

    def pair_batch(b, between):
        pairs, scales = [], []
        for k in range(2):
            entries = {(pl_, pc_): PAIRS[pl_][pc_][b][k] for pl_ in (0, 1) for pc_ in (0, 1)}

            def value(field):
                return pick({key: field(entry) for key, entry in entries.items()})

            phase = (value(lambda t: int(t[4] == 0)) * (at.z // 2)
                     + value(lambda t: int(t[4] == 1)) * (at.y // 2))

            def both(field):
                v0 = value(lambda t: field(t, 0))
                return v0 + phase * (value(lambda t: field(t, 1)) - v0)

            p = both(lambda t, w: t[2 * w])
            q = both(lambda t, w: t[2 * w + 1])

            def band_of(which):
                def part(axis):
                    def get(host_l, t, w):
                        index = t[2 * w + which]
                        if index == 0:
                            return 0
                        element = ELEMENTS[host_l][index - 1]
                        return element[1 if (element[2] is not None and w == 1) else 0][axis]

                    def table_of(w):
                        return pick({key: get(key[0], entry, w) for key, entry in entries.items()})

                    v0 = table_of(0)
                    return v0 + phase * (table_of(1) - v0)

                z = (at.z + part(0)) % 4
                y = (at.y + part(1)) % 4
                h = (at.h + part(2)) % 2
                return (z * 4 + y) * 2 + h

            weight = keep_at(band_of(0), band_of(1))
            unused = value(lambda t: int(t[5])) * at.h
            pairs.append((p, q))
            scales.append(weight * (jnp.int32(1) - unused).astype(F32))

        def update(lanes, v0, v1):
            for (p, q), scale, v in zip(pairs, scales, (v0, v1)):
                scaled = scale * v
                to_p = scaled * slots[q, :, lanes]
                to_q = scaled * slots[p, :, lanes]
                for target, term in ((p, to_p), (q, to_q)):
                    for s in range(4):
                        acc[target, s % 2, s // 2, :, lanes] += term[16 * s : 16 * s + 16]

        transform(pairs, update, between)

    def exchange(e):
        return pltpu.make_async_remote_copy(
            src_ref=acc.at[e, 1 - c], dst_ref=xbuf.at[e],
            send_sem=x_send.at[e], recv_sem=x_recv.at[e], device_id=sibling, device_id_type=MESH)

    def send_back(host_l, e, u, there):
        return pltpu.make_async_remote_copy(
            src_ref=acc.at[e + 1, c], dst_ref=rbuf.at[host_l * K + e],
            send_sem=r_send.at[e], recv_sem=r_recv.at[host_l * K + e],
            device_id=(at.band_at(u, 1), 2 * there + c), device_id_type=MESH)

    def return_all(chosen):
        for host_l in (0, 1):
            mine = chosen[host_l]

            @pl.when(l == host_l)
            def _():
                for e in mine:
                    exchange(e + 1).start()

        for host_l in (0, 1):
            mine = chosen[host_l]

            @pl.when(l == host_l)
            def _():
                for e in mine:
                    exchange(e + 1).wait_recv()
                    acc[e + 1, c] += xbuf[e + 1]
                    for w_l, w_e, u, there, condition in want_list:
                        if (w_l, w_e) == (host_l, e):

                            @pl.when(condition)
                            def _():
                                send_back(w_l, w_e, u, there).start()

    table_copy.wait()
    for_elements(True, pass_on)
    transform([(0, 0), (0, 0)], self_update, lambda: None)
    for_elements(True, pass_done)
    pair_batch(0, lambda: for_elements(False, pass_on))
    for_elements(False, pass_done)
    return_all(EARLY_BACK)
    pair_batch(1, lambda: None)
    exchange(0).start()
    return_all(LATE_BACK)
    exchange(0).wait_recv()
    acc[0, c] += xbuf[0]

    for host_l, e, u, condition in host_list:

        @pl.when(condition)
        def _():
            send_back(host_l, e, u, 0).wait_recv()
            acc[0, c] += rbuf[host_l * K + e]

    swap = pltpu.make_async_remote_copy(
        src_ref=acc.at[0, c, 1 - l], dst_ref=fbuf, send_sem=s_sem.at[0], recv_sem=s_sem.at[1],
        device_id=twin, device_id_type=MESH)
    swap.start()
    swap.wait()
    out_ref[...] = acc[0, c, l] + fbuf[...]

    exchange(0).wait_send()
    for host_l, e, u, condition in host_list:

        @pl.when(condition)
        def _():
            orbital_out(host_l, e, u).wait_send()

    for host_l, e, u, there, condition in want_list:

        @pl.when(condition)
        def _():
            exchange(e + 1).wait_send()
            send_back(host_l, e, u, there).wait_send()


def body(orbitals, pair_keep, wz, wr, table):
    dma = pltpu.SemaphoreType.DMA
    out = pl.pallas_call(
        kernel,
        name="exchange",
        out_shape=jax.ShapeDtypeStruct((16, NYZ), F32),
        in_specs=[
            pl.BlockSpec(memory_space=pl.ANY),
            pl.BlockSpec(memory_space=pltpu.SMEM),
            pl.BlockSpec(memory_space=pltpu.VMEM),
            pl.BlockSpec(memory_space=pltpu.VMEM),
            pl.BlockSpec(memory_space=pl.ANY),
        ],
        out_specs=pl.BlockSpec(memory_space=pltpu.VMEM),
        scratch_shapes=[
            pltpu.VMEM((K + 1, NX, NYZ), F32),
            pltpu.VMEM((K + 1, 2, 2, 16, NYZ), F32),
            pltpu.VMEM((K + 1, 2, 16, NYZ), F32),
            pltpu.VMEM((2 * K, 2, 16, NYZ), F32),
            pltpu.VMEM((16, NYZ), F32),
            pltpu.VMEM((64 * 64, 128), F32),
            pltpu.VMEM((64, 64, 128), F32),
            dma((2,)),
            dma((2 * K,)), dma((K,)),
            dma((K,)), dma((K,)),
            dma((K + 1,)), dma((K + 1,)),
            dma((K,)), dma((2 * K,)),
            dma((2,)),
        ],
        compiler_params=pltpu.CompilerParams(
            collective_id=0, has_side_effects=True, vmem_limit_bytes=56 << 20),
    )(orbitals.reshape(NX, NYZ), pair_keep, wz, wr, table)
    return out.reshape(1, 16, NYZ)


def solution(mesh):
    constants = (lane_matrix(), sublane_matrix(), screened_table())

    def call(orbitals, pair_keep):
        return body(orbitals, pair_keep, *[jnp.asarray(x) for x in constants])

    return jax.shard_map(
        call,
        mesh=mesh,
        in_specs=(P("band", None, None), P()),
        out_specs=P("band", "pair", None),
        check_vma=False,
    )
```

```python
import functools
import math

import jax
import jax.numpy as jnp
import ml_dtypes
import numpy as np
from jax import lax
from jax.experimental import pallas as pl
from jax.experimental.pallas import tpu as pltpu
from jax.sharding import PartitionSpec as P

NX = NY = NZ = 64
NYZ = NY * NZ
CELL_LENGTH = 46.92
SCREEN_OMEGA = 0.11
BF16 = jnp.bfloat16
F32 = jnp.float32
MESH = pl.DeviceIdType.MESH

ELEMENTS = [[((0, 3, 0), (0, 3, 0), 0, None), ((1, 0, 1), (1, 0, 1), 0, None), ((3, 1, 0), (3, 1, 0), 0, None), ((0, 0, 1), (0, 0, 1), 0, None), ((1, 0, 0), (1, 0, 0), 0, None)], [((0, 2, 0), (0, 2, 0), 0, None), ((2, 0, 0), (2, 0, 1), 1, None), ((1, 0, 1), (1, 0, 1), 0, ((0, 0, 0), 0, 2)), ((3, 0, 0), (3, 0, 0), 0, None), ((0, 0, 1), (0, 0, 1), 0, None)]]
EARLY_NEAR = [[0, 1, 2], [0, 1]]
EARLY_FAR = [[], [2]]
LATE_NEAR = [[3, 4], [3, 4]]
LATE_FAR = [[], []]
BACK_EARLY = [[], [1, 2]]
BACK_EARLY_JOIN = [[1], []]
BACK_LATE = [[0, 2, 3, 4], [0, 3, 4]]
BACK_LATE_JOIN = [[], []]
PAIRS = [[[[(1, 0, 1, 0, 0, 0), (2, 3, 2, 3, 0, 0)], [(1, 4, 1, 4, 0, 0), (3, 4, 3, 4, 0, 0)]], [[(1, 2, 1, 2, 0, 0), (3, 0, 3, 0, 0, 0)], [(1, 5, 1, 5, 0, 0), (5, 3, 5, 3, 0, 0)]]], [[[(0, 2, 0, 2, 1, 0), (1, 2, 1, 2, 1, 0)], [(4, 0, 4, 0, 0, 0), (4, 5, 4, 5, 0, 0)]], [[(1, 3, 1, 3, 0, 0), (1, 0, 1, 0, 0, 2)], [(4, 1, 4, 1, 0, 0), (5, 1, 5, 0, 5, 0)]]]]
K = max(len(ELEMENTS[0]), len(ELEMENTS[1]))
JC = 8
YC = 2 * JC
CHUNK = 128 * JC


def cas_matrix():
    counter = np.arange(64)
    angles = 2.0 * math.pi * (np.outer(counter, counter) % 64) / 64
    return np.cos(angles) + np.sin(angles)


def split_constant(matrix):
    high = matrix.astype(ml_dtypes.bfloat16)
    low = (matrix - high.astype(np.float64)).astype(ml_dtypes.bfloat16)
    return high, low


def lane_matrix():
    high, low = split_constant(np.kron(np.eye(2), cas_matrix()))
    row = np.concatenate([high, low], axis=1)
    return np.concatenate([row, row], axis=0)


def sublane_matrix():
    high, low = split_constant(cas_matrix())
    return np.concatenate([np.concatenate([high, high], 1), np.concatenate([low, low], 1)], 0)


def screened_table():
    counter = np.arange(64)
    wave = np.minimum(counter, 64 - counter) * (2.0 * math.pi / CELL_LENGTH)
    square = wave[:, None, None] ** 2 + wave[None, :, None] ** 2 + wave[None, None, :] ** 2
    guarded = np.where(square > 0.0, square, 1.0)
    screened = 4.0 * math.pi / guarded * -np.expm1(-guarded / (4.0 * SCREEN_OMEGA**2))
    table = np.where(square > 0.0, screened, 0.0) * (-1.0 / (NX * NY * NZ))
    return np.concatenate([table, table], axis=2).astype(np.float32)


def dot(a, b):
    return jnp.dot(a, b, preferred_element_type=F32)


def halves(v):
    high = v.astype(BF16)
    low = (v - high.astype(F32)).astype(BF16)
    return high, low


def along_lanes(v, weights):
    out = dot(jnp.concatenate(halves(v), axis=1), weights)
    return out[:, :128] + out[:, 128:]


def along_rows(v, weights):
    out = dot(weights, jnp.concatenate(halves(v), axis=0))
    return out[:64] + out[64:]


def rows_to_lanes(v, count):
    return jnp.concatenate([v[64 * i : 64 * i + 64] for i in range(count)], axis=1)


def lanes_to_rows(v, count):
    return jnp.concatenate([v[:, 128 * i : 128 * i + 128] for i in range(count)], axis=0)


class Place:
    def __init__(self):
        band = lax.axis_index("band")
        pair = lax.axis_index("pair")
        self.z, self.y, self.h = band // 8, (band // 2) % 4, band % 2
        self.l, self.c = pair // 2, pair % 2
        self.band = band

    def shifted(self, u, sign):
        z = (self.z + 4 + sign * u[0]) % 4
        y = (self.y + 4 + sign * u[1]) % 4
        h = (self.h + u[2]) % 2
        return z, y, h

    def band_at(self, u, sign):
        z, y, h = self.shifted(u, sign)
        return (z * 4 + y) * 2 + h

    def phase_at(self, mask, u, sign):
        z, y, h = self.shifted(u, sign)
        bits = (z // 2, y // 2, h)
        return sum(bit for k, bit in enumerate(bits) if mask >> k & 1) % 2


class Transfer:
    def __init__(self, place, l, e, step, from_l, slot, mask=0, value=0):
        self.l, self.e, self.step, self.from_l, self.slot = l, e, step, from_l, slot
        self.here, self.mine = place.l == from_l, place.l == l
        if mask:
            self.here = self.here & (place.phase_at(mask, step, -1) == value)
            self.mine = self.mine & (place.phase_at(mask, (0, 0, 0), 1) == value)


def transfers(place):
    found = []
    for l in (0, 1):
        for e, (first, second, mask, relay) in enumerate(ELEMENTS[l]):
            if relay is not None:
                found.append(Transfer(place, l, e, *relay))
                continue
            for value, u in enumerate((first, second) if mask else (first,)):
                from_l = l if u[2] == 0 else 1 - l
                found.append(Transfer(place, l, e, u, from_l, 0, mask, value))
    return found


def kernel(orb_ref, keep_ref, wz_ref, wr_ref, table_hbm, out_ref,
           slots, acc, xbuf, rbuf, fbuf, spect, table,
           local_sem, d_send, d_recv, f_send, f_recv, x_send, x_recv, r_send, r_recv, s_send, s_recv):
    at = Place()
    l, c = at.l, at.c
    sibling = (at.band, 2 * l + 1 - c)
    twin = (at.band, 2 * (1 - l) + c)

    def pick(values):
        out = 0
        for (pl_, pc_), value in values.items():
            if value != 0:
                out = out + value * ((l == pl_) & (c == pc_)).astype(jnp.int32)
        return out

    own_copy = pltpu.make_async_copy(orb_ref, slots.at[0], local_sem.at[0])
    own_copy.start()
    table_copy = pltpu.make_async_copy(table_hbm, table, local_sem.at[1])
    table_copy.start()

    barrier = pltpu.get_barrier_semaphore()
    peers = 2
    pl.semaphore_signal(barrier, inc=1, device_id=sibling, device_id_type=MESH)
    pl.semaphore_signal(barrier, inc=1, device_id=twin, device_id_type=MESH)
    moves = transfers(at)

    def child(move):
        return (at.band_at(move.step, -1), 2 * move.l + c)

    def parent(move):
        return (at.band_at(move.step, 1), 2 * move.from_l + c)

    for move in moves:
        peers = peers + move.here.astype(jnp.int32) + move.mine.astype(jnp.int32)

        @pl.when(move.here)
        def _():
            pl.semaphore_signal(barrier, inc=1, device_id=child(move), device_id_type=MESH)

        @pl.when(move.mine)
        def _():
            pl.semaphore_signal(barrier, inc=1, device_id=parent(move), device_id_type=MESH)

    for e in range(1, K + 1):
        acc[e] = jnp.zeros(acc.shape[1:], F32)
    own_copy.wait()
    pl.semaphore_wait(barrier, peers)

    my_rows = pl.ds(pl.multiple_of(32 * c, 32), 32)

    def chunk(i):
        return pl.ds(pl.multiple_of(i * CHUNK, CHUNK), CHUNK)

    everything = pl.ds(0, NYZ)

    def orbital_out(move, lanes, i=0):
        return pltpu.make_async_remote_copy(
            src_ref=slots.at[move.slot, my_rows, lanes],
            dst_ref=slots.at[move.e + 1, my_rows, lanes],
            send_sem=d_send.at[move.l * K + move.e], recv_sem=d_recv.at[move.e * 4 + i],
            device_id=child(move), device_id_type=MESH)

    def is_early(move):
        return move.e in EARLY_NEAR[move.l] or move.e in EARLY_FAR[move.l]

    for early in (True, False):
        for i in range(4):
            for move in moves:
                if move.slot == 0 and is_early(move) == early:

                    @pl.when(move.here)
                    def _():
                        orbital_out(move, chunk(i), i).start()

    def forward(e, lanes, i=0):
        return pltpu.make_async_remote_copy(
            src_ref=slots.at[e + 1, my_rows, lanes], dst_ref=slots.at[e + 1, my_rows, lanes],
            send_sem=f_send.at[e], recv_sem=f_recv.at[e * 4 + i],
            device_id=sibling, device_id_type=MESH)

    def for_chip(chosen, body):
        for chip in (0, 1):
            if chosen[chip]:

                @pl.when(l == chip)
                def _():
                    for e in chosen[chip]:
                        body(chip, e)

    def pass_on(chosen, i):
        def one(chip, e):
            arriving = [move for move in moves if (move.l, move.e) == (chip, e)][0]
            orbital_out(arriving, chunk(i), i).wait_recv()
            forward(e, chunk(i), i).start()
            for move in moves:
                if (move.from_l, move.slot) == (chip, e + 1):
                    orbital_out(move, chunk(i), i).start()

        for_chip(chosen, one)

    def passed_on(chosen, i):
        for_chip(chosen, lambda chip, e: forward(e, chunk(i), i).wait_recv())

    low_lanes = lax.broadcasted_iota(jnp.int32, (64, 128), 1) < 64

    def lanes_of(i):
        return chunk(i)

    def transform(pairs, update, before=None, middle=None, after=None):
        wz, wr = wz_ref[...], wr_ref[...]
        (p0, q0), (p1, q1) = pairs

        def first(i, carry):
            if before is not None:
                before(i)
            lanes = lanes_of(i)
            d0 = slots[p0, :, lanes] * slots[q0, :, lanes]
            d1 = slots[p1, :, lanes] * slots[q1, :, lanes]
            tiles = []
            for j in range(JC):
                t0, t1 = d0[:, 128 * j : 128 * j + 128], d1[:, 128 * j : 128 * j + 128]
                tiles.append(jnp.where(low_lanes, t0, pltpu.roll(t1, 64, 1)))
                tiles.append(jnp.where(low_lanes, pltpu.roll(t0, 64, 1), t1))
            v = along_lanes(jnp.concatenate(tiles, axis=0), wz)
            v = along_rows(rows_to_lanes(v, YC), wr)
            spect[pl.ds(pl.multiple_of(i * (64 * YC), 64 * YC), 64 * YC), :] = lanes_to_rows(v, YC)
            return carry

        def second(i, carry):
            if middle is not None:
                middle(i)
            rows = [pl.ds(i * YC + k, 64, stride=64) for k in range(YC)]
            v = along_rows(jnp.concatenate([spect[r, :] for r in rows], axis=1), wr)
            scale = jnp.concatenate([table[i * YC + k] for k in range(YC)], axis=1)
            v = along_rows(v * scale, wr)
            for k in range(YC):
                spect[rows[k], :] = v[:, 128 * k : 128 * k + 128]
            return carry

        def third(i, carry):
            v = spect[pl.ds(pl.multiple_of(i * (64 * YC), 64 * YC), 64 * YC), :]
            v = along_rows(rows_to_lanes(v, YC), wr)
            v = along_lanes(lanes_to_rows(v, YC), wz)
            v0, v1 = [], []
            for j in range(JC):
                even, odd = v[128 * j : 128 * j + 64], v[128 * j + 64 : 128 * j + 128]
                v0.append(jnp.where(low_lanes, even, pltpu.roll(odd, 64, 1)))
                v1.append(jnp.where(low_lanes, pltpu.roll(even, 64, 1), odd))
            update(lanes_of(i), jnp.concatenate(v0, axis=1), jnp.concatenate(v1, axis=1))
            if after is not None:
                after(i)
            return carry

        lax.fori_loop(0, 64 // YC, first, 0)
        lax.fori_loop(0, 64 // YC, second, 0)
        lax.fori_loop(0, 64 // YC, third, 0)

    def keep_at(i, j):
        return keep_ref[i, j].astype(F32)

    self_keep = keep_at(at.band, at.band)

    def self_update(lanes, v0, v1):
        orbital = slots[0, :, lanes]
        for s in range(4):
            rows = slice(16 * s, 16 * s + 16)
            mine = self_keep * (2 * l + c == s).astype(F32)
            acc[0, s % 2, s // 2, :, lanes] = (mine * v0[rows]) * orbital[rows]

    def pair_batch(b, before, middle, after):
        pairs, scales = [], []
        for k in range(2):
            entries = {(pl_, pc_): PAIRS[pl_][pc_][b][k] for pl_ in (0, 1) for pc_ in (0, 1)}

            def value(field):
                return pick({key: field(entry) for key, entry in entries.items()})

            bits = (at.z // 2, at.y // 2, at.h)
            phase = sum(value(lambda t: t[4] >> n & 1) * bits[n] for n in range(3)) % 2
            unused = sum(value(lambda t: t[5] >> n & 1) * bits[n] for n in range(3)) % 2

            def both(field):
                v0 = value(lambda t: field(t, 0))
                return v0 + phase * (value(lambda t: field(t, 1)) - v0)

            p = both(lambda t, w: t[2 * w])
            q = both(lambda t, w: t[2 * w + 1])

            def band_of(which):
                def part(axis):
                    def get(host_l, t, w):
                        index = t[2 * w + which]
                        if index == 0:
                            return 0
                        element = ELEMENTS[host_l][index - 1]
                        return element[1 if (element[2] and w == 1) else 0][axis]

                    def table_of(w):
                        return pick({key: get(key[0], entry, w) for key, entry in entries.items()})

                    v0 = table_of(0)
                    return v0 + phase * (table_of(1) - v0)

                z = (at.z + part(0)) % 4
                y = (at.y + part(1)) % 4
                h = (at.h + part(2)) % 2
                return (z * 4 + y) * 2 + h

            weight = keep_at(band_of(0), band_of(1))
            pairs.append((p, q))
            scales.append(weight * (jnp.int32(1) - unused).astype(F32))

        def update(lanes, v0, v1):
            for (p, q), scale, v in zip(pairs, scales, (v0, v1)):
                scaled = scale * v
                to_p = scaled * slots[q, :, lanes]
                to_q = scaled * slots[p, :, lanes]
                for target, term in ((p, to_p), (q, to_q)):
                    for s in range(4):
                        acc[target, s % 2, s // 2, :, lanes] += term[16 * s : 16 * s + 16]

        transform(pairs, update, before, middle, after)

    def exchange(e, lanes, i=0):
        return pltpu.make_async_remote_copy(
            src_ref=acc.at[e, 1 - c, :, :, lanes], dst_ref=xbuf.at[e, :, :, lanes],
            send_sem=x_send.at[e], recv_sem=x_recv.at[e * 4 + i],
            device_id=sibling, device_id_type=MESH)

    def send_back(move, lanes, i=0):
        return pltpu.make_async_remote_copy(
            src_ref=acc.at[move.e + 1, c, :, :, lanes],
            dst_ref=rbuf.at[move.l * K + move.e, :, :, lanes],
            send_sem=r_send.at[move.e], recv_sem=r_recv.at[(move.l * K + move.e) * 4 + i],
            device_id=parent(move), device_id_type=MESH)

    def swap(lanes, i=0):
        return pltpu.make_async_remote_copy(
            src_ref=acc.at[0, c, 1 - l, :, lanes], dst_ref=fbuf.at[:, lanes],
            send_sem=s_send.at[0], recv_sem=s_recv.at[i], device_id=twin, device_id_type=MESH)

    def start_return(chosen, i):
        for_chip(chosen, lambda chip, e: exchange(e + 1, chunk(i), i).start())

    def collect(move, e, lanes, i):
        send_back(move, lanes, i).wait_recv()
        acc[e, c, :, :, lanes] += rbuf[move.l * K + move.e, :, :, lanes]

    def finish_return(chosen, i):
        lanes = chunk(i)

        def one(chip, e):
            exchange(e + 1, lanes, i).wait_recv()
            acc[e + 1, c, :, :, lanes] += xbuf[e + 1, :, :, lanes]
            for move in moves:
                if (move.from_l, move.slot) == (chip, e + 1):
                    collect(move, e + 1, lanes, i)
            for move in moves:
                if (move.l, move.e) == (chip, e):

                    @pl.when(move.mine)
                    def _():
                        send_back(move, lanes, i).start()

        for_chip(chosen, one)

    def at_step(i, step, *actions):
        @pl.when(i == step)
        def _():
            for action, *arguments in actions:
                action(*arguments)

    def first_before(i):
        at_step(i, 1, (pass_on, EARLY_FAR, 1))
        at_step(i, 2, (pass_on, EARLY_NEAR, 3), (pass_on, EARLY_FAR, 2))
        at_step(i, 3, (pass_on, EARLY_FAR, 3))
        passed_on(EARLY_NEAR, i)
        passed_on(EARLY_FAR, i)

    def first_middle(i):
        at_step(i, 0, (pass_on, LATE_NEAR, 0))

    def first_after(i):
        start_return(BACK_EARLY, i)
        start_return(BACK_EARLY_JOIN, i)

        @pl.when(i > 0)
        def _():
            finish_return(BACK_EARLY, i - 1)
            pass_on(LATE_NEAR, i)

    def second_before(i):
        pass_on(LATE_FAR, i)
        passed_on(LATE_NEAR, i)
        passed_on(LATE_FAR, i)

    def second_after(i):
        start_return(BACK_LATE, i)
        start_return(BACK_LATE_JOIN, i)
        exchange(0, chunk(i), i).start()
        finish_return(BACK_EARLY_JOIN, i)

        @pl.when(i > 0)
        def _():
            finish_return(BACK_LATE, i - 1)

    table_copy.wait()
    transform([(0, 0), (0, 0)], self_update)
    pass_on(EARLY_NEAR, 0)
    pass_on(EARLY_NEAR, 1)
    pass_on(EARLY_FAR, 0)
    pass_on(EARLY_NEAR, 2)
    pair_batch(0, first_before, first_middle, first_after)
    finish_return(BACK_EARLY, 3)
    pair_batch(1, second_before, None, second_after)
    finish_return(BACK_LATE, 3)

    def gather(i, carry):
        lanes = chunk(i)
        finish_return(BACK_LATE_JOIN, i)
        exchange(0, lanes, i).wait_recv()
        acc[0, c, :, :, lanes] += xbuf[0, :, :, lanes]
        for move in moves:
            if move.slot == 0:

                @pl.when(move.here)
                def _():
                    collect(move, 0, lanes, i)

        swap(lanes, i).start()
        return carry

    def finish(i, carry):
        lanes = chunk(i)
        swap(lanes, i).wait_recv()
        out_ref[:, lanes] = acc[0, c, l, :, lanes] + fbuf[:, lanes]
        return carry

    lax.fori_loop(0, 4, gather, 0)
    lax.fori_loop(0, 4, finish, 0)

    swap(everything).wait_send()
    exchange(0, everything).wait_send()
    elements = [range(len(ELEMENTS[0])), range(len(ELEMENTS[1]))]
    for_chip(elements, lambda chip, e: forward(e, everything).wait_send())
    for_chip(elements, lambda chip, e: exchange(e + 1, everything).wait_send())
    for move in moves:

        @pl.when(move.here)
        def _():
            orbital_out(move, everything).wait_send()

        @pl.when(move.mine)
        def _():
            send_back(move, everything).wait_send()


def body(orbitals, pair_keep, wz, wr, table):
    dma = pltpu.SemaphoreType.DMA
    out = pl.pallas_call(
        kernel,
        name="exchange",
        out_shape=jax.ShapeDtypeStruct((16, NYZ), F32),
        in_specs=[
            pl.BlockSpec(memory_space=pl.ANY),
            pl.BlockSpec(memory_space=pltpu.SMEM),
            pl.BlockSpec(memory_space=pltpu.VMEM),
            pl.BlockSpec(memory_space=pltpu.VMEM),
            pl.BlockSpec(memory_space=pl.ANY),
        ],
        out_specs=pl.BlockSpec(memory_space=pltpu.VMEM),
        scratch_shapes=[
            pltpu.VMEM((K + 1, NX, NYZ), F32),
            pltpu.VMEM((K + 1, 2, 2, 16, NYZ), F32),
            pltpu.VMEM((K + 1, 2, 16, NYZ), F32),
            pltpu.VMEM((2 * K, 2, 16, NYZ), F32),
            pltpu.VMEM((16, NYZ), F32),
            pltpu.VMEM((64 * 64, 128), F32),
            pltpu.VMEM((64, 64, 128), F32),
            dma((2,)),
            dma((2 * K,)), dma((4 * K,)),
            dma((K,)), dma((4 * K,)),
            dma((K + 1,)), dma((4 * K + 4,)),
            dma((K,)), dma((8 * K,)),
            dma((1,)), dma((4,)),
        ],
        compiler_params=pltpu.CompilerParams(
            collective_id=0, has_side_effects=True, vmem_limit_bytes=56 << 20),
    )(orbitals.reshape(NX, NYZ), pair_keep, wz, wr, table)
    return out.reshape(1, 16, NYZ)


def solution(mesh):
    constants = (lane_matrix(), sublane_matrix(), screened_table())

    def call(orbitals, pair_keep):
        return body(orbitals, pair_keep, *[jnp.asarray(x) for x in constants])

    return jax.shard_map(
        call,
        mesh=mesh,
        in_specs=(P("band", None, None), P()),
        out_specs=P("band", "pair", None),
        check_vma=False,
    )
```

```python
import functools
import math

import jax
import jax.numpy as jnp
import ml_dtypes
import numpy as np
from jax import lax
from jax.experimental import pallas as pl
from jax.experimental.pallas import tpu as pltpu
from jax.sharding import PartitionSpec as P

NX = NY = NZ = 64
NYZ = NY * NZ
CELL_LENGTH = 46.92
SCREEN_OMEGA = 0.11
BF16 = jnp.bfloat16
F32 = jnp.float32
MESH = pl.DeviceIdType.MESH

ELEMENTS = [[((0, 2, 0), (0, 2, 0), 0, None), ((2, 0, 1), (2, 0, 0), 1, None), ((3, 1, 0), (3, 1, 0), 0, ((0, 0, 0), 1, 3)), ((3, 0, 0), (3, 0, 0), 0, None), ((0, 0, 1), (0, 0, 1), 0, None)], [((0, 3, 0), (0, 3, 0), 0, None), ((1, 0, 1), (1, 0, 1), 0, None), ((3, 1, 0), (3, 1, 0), 0, None), ((0, 2, 0), (0, 2, 0), 0, ((0, 0, 0), 0, 1)), ((0, 0, 1), (0, 0, 1), 0, None), ((1, 0, 0), (1, 0, 0), 0, None)]]
EARLY_NEAR = [[0, 1], [0, 1, 2]]
EARLY_FAR = [[2], [3]]
LATE_NEAR = [[3, 4], [4, 5]]
LATE_FAR = [[], []]
BACK_EARLY = [[1, 2], [1, 3]]
BACK_EARLY_JOIN = [[], []]
BACK_LATE = [[0, 3, 4], [0, 2, 4, 5]]
BACK_LATE_JOIN = [[], []]
PAIRS = [[[[(3, 1, 3, 1, 0, 0), (1, 2, 1, 2, 1, 0)], [(4, 5, 4, 5, 0, 0), (1, 0, 1, 5, 3, 0)]], [[(3, 0, 3, 0, 0, 0), (0, 2, 0, 2, 1, 0)], [(4, 1, 4, 1, 0, 0), (5, 0, 5, 0, 0, 4)]]], [[[(1, 2, 1, 2, 0, 0), (2, 3, 2, 3, 0, 0)], [(1, 5, 1, 5, 0, 0), (0, 6, 0, 6, 0, 0)]], [[(1, 0, 1, 0, 0, 0), (4, 2, 4, 2, 0, 0)], [(3, 5, 3, 5, 0, 0), (6, 3, 6, 3, 0, 0)]]]]
K = max(len(ELEMENTS[0]), len(ELEMENTS[1]))
JC = 8
YC = 2 * JC
CHUNK = 128 * JC


def cas_matrix():
    counter = np.arange(64)
    angles = 2.0 * math.pi * (np.outer(counter, counter) % 64) / 64
    return np.cos(angles) + np.sin(angles)


def split_constant(matrix):
    high = matrix.astype(ml_dtypes.bfloat16)
    low = (matrix - high.astype(np.float64)).astype(ml_dtypes.bfloat16)
    return high, low


def lane_matrix():
    high, low = split_constant(np.kron(np.eye(2), cas_matrix()))
    row = np.concatenate([high, low], axis=1)
    return np.concatenate([row, row], axis=0)


def sublane_matrix():
    high, low = split_constant(cas_matrix())
    return np.concatenate([np.concatenate([high, high], 1), np.concatenate([low, low], 1)], 0)


def screened_table():
    counter = np.arange(64)
    wave = np.minimum(counter, 64 - counter) * (2.0 * math.pi / CELL_LENGTH)
    square = wave[:, None, None] ** 2 + wave[None, :, None] ** 2 + wave[None, None, :] ** 2
    guarded = np.where(square > 0.0, square, 1.0)
    screened = 4.0 * math.pi / guarded * -np.expm1(-guarded / (4.0 * SCREEN_OMEGA**2))
    table = np.where(square > 0.0, screened, 0.0) * (-1.0 / (NX * NY * NZ))
    return np.concatenate([table, table], axis=2).astype(np.float32)


def dot(a, b):
    return jnp.dot(a, b, preferred_element_type=F32)


def halves(v):
    high = v.astype(BF16)
    low = (v - high.astype(F32)).astype(BF16)
    return high, low


def along_lanes(v, weights):
    out = dot(jnp.concatenate(halves(v), axis=1), weights)
    return out[:, :128] + out[:, 128:]


def along_rows(v, weights):
    out = dot(weights, jnp.concatenate(halves(v), axis=0))
    return out[:64] + out[64:]


def rows_to_lanes(v, count):
    return jnp.concatenate([v[64 * i : 64 * i + 64] for i in range(count)], axis=1)


def lanes_to_rows(v, count):
    return jnp.concatenate([v[:, 128 * i : 128 * i + 128] for i in range(count)], axis=0)


class Place:
    def __init__(self):
        band = lax.axis_index("band")
        pair = lax.axis_index("pair")
        self.z, self.y, self.h = band // 8, (band // 2) % 4, band % 2
        self.l, self.c = pair // 2, pair % 2
        self.band = band

    def shifted(self, u, sign):
        z = (self.z + 4 + sign * u[0]) % 4
        y = (self.y + 4 + sign * u[1]) % 4
        h = (self.h + u[2]) % 2
        return z, y, h

    def band_at(self, u, sign):
        z, y, h = self.shifted(u, sign)
        return (z * 4 + y) * 2 + h

    def phase_at(self, mask, u, sign):
        z, y, h = self.shifted(u, sign)
        bits = (z // 2, y // 2, h)
        return sum(bit for k, bit in enumerate(bits) if mask >> k & 1) % 2


class Transfer:
    def __init__(self, place, l, e, step, from_l, slot, mask=0, value=0):
        self.l, self.e, self.step, self.from_l, self.slot = l, e, step, from_l, slot
        self.here, self.mine = place.l == from_l, place.l == l
        if mask:
            self.here = self.here & (place.phase_at(mask, step, -1) == value)
            self.mine = self.mine & (place.phase_at(mask, (0, 0, 0), 1) == value)


def transfers(place):
    found = []
    for l in (0, 1):
        for e, (first, second, mask, relay) in enumerate(ELEMENTS[l]):
            if relay is not None:
                found.append(Transfer(place, l, e, *relay))
                continue
            for value, u in enumerate((first, second) if mask else (first,)):
                from_l = l if u[2] == 0 else 1 - l
                found.append(Transfer(place, l, e, u, from_l, 0, mask, value))
    return found


def kernel(orb_ref, keep_ref, wz_ref, wr_ref, table_hbm, out_ref,
           slots, acc, xbuf, rbuf, fbuf, spect, table,
           local_sem, d_send, d_recv, f_send, f_recv, x_send, x_recv, r_send, r_recv, s_send, s_recv):
    at = Place()
    l, c = at.l, at.c
    sibling = (at.band, 2 * l + 1 - c)
    twin = (at.band, 2 * (1 - l) + c)

    def pick(values):
        out = 0
        for (pl_, pc_), value in values.items():
            if value != 0:
                out = out + value * ((l == pl_) & (c == pc_)).astype(jnp.int32)
        return out

    own_copy = pltpu.make_async_copy(orb_ref, slots.at[0], local_sem.at[0])
    own_copy.start()
    table_copy = pltpu.make_async_copy(table_hbm, table, local_sem.at[1])
    table_copy.start()

    barrier = pltpu.get_barrier_semaphore()
    peers = 2
    pl.semaphore_signal(barrier, inc=1, device_id=sibling, device_id_type=MESH)
    pl.semaphore_signal(barrier, inc=1, device_id=twin, device_id_type=MESH)
    moves = transfers(at)

    def child(move):
        return (at.band_at(move.step, -1), 2 * move.l + c)

    def parent(move):
        return (at.band_at(move.step, 1), 2 * move.from_l + c)

    for move in moves:
        peers = peers + move.here.astype(jnp.int32) + move.mine.astype(jnp.int32)

        @pl.when(move.here)
        def _():
            pl.semaphore_signal(barrier, inc=1, device_id=child(move), device_id_type=MESH)

        @pl.when(move.mine)
        def _():
            pl.semaphore_signal(barrier, inc=1, device_id=parent(move), device_id_type=MESH)

    own_copy.wait()
    pl.semaphore_wait(barrier, peers)

    my_rows = pl.ds(pl.multiple_of(32 * c, 32), 32)

    def chunk(i):
        return pl.ds(pl.multiple_of(i * CHUNK, CHUNK), CHUNK)

    everything = pl.ds(0, NYZ)

    def orbital_out(move, lanes, i=0):
        return pltpu.make_async_remote_copy(
            src_ref=slots.at[move.slot, my_rows, lanes],
            dst_ref=slots.at[move.e + 1, my_rows, lanes],
            send_sem=d_send.at[move.l * K + move.e], recv_sem=d_recv.at[move.e * 4 + i],
            device_id=child(move), device_id_type=MESH)

    def is_early(move):
        return move.e in EARLY_NEAR[move.l] or move.e in EARLY_FAR[move.l]

    for early in (True, False):
        for i in range(4):
            for move in moves:
                if move.slot == 0 and is_early(move) == early:

                    @pl.when(move.here)
                    def _():
                        orbital_out(move, chunk(i), i).start()

    for e in range(1, K + 1):
        acc[e] = jnp.zeros(acc.shape[1:], F32)

    def forward(e, lanes, i=0):
        return pltpu.make_async_remote_copy(
            src_ref=slots.at[e + 1, my_rows, lanes], dst_ref=slots.at[e + 1, my_rows, lanes],
            send_sem=f_send.at[e], recv_sem=f_recv.at[e * 4 + i],
            device_id=sibling, device_id_type=MESH)

    def for_chip(chosen, body):
        for chip in (0, 1):
            if chosen[chip]:

                @pl.when(l == chip)
                def _():
                    for e in chosen[chip]:
                        body(chip, e)

    def pass_on(chosen, i):
        def one(chip, e):
            arriving = [move for move in moves if (move.l, move.e) == (chip, e)][0]
            orbital_out(arriving, chunk(i), i).wait_recv()
            forward(e, chunk(i), i).start()
            for move in moves:
                if (move.from_l, move.slot) == (chip, e + 1):
                    orbital_out(move, chunk(i), i).start()

        for_chip(chosen, one)

    def passed_on(chosen, i):
        for_chip(chosen, lambda chip, e: forward(e, chunk(i), i).wait_recv())

    low_lanes = lax.broadcasted_iota(jnp.int32, (64, 128), 1) < 64

    def lanes_of(i):
        return chunk(i)

    def transform(pairs, update, before=None, middle=None, after=None):
        wz, wr = wz_ref[...], wr_ref[...]
        (p0, q0), (p1, q1) = pairs

        def first(i, carry):
            if before is not None:
                before(i)
            lanes = lanes_of(i)
            d0 = slots[p0, :, lanes] * slots[q0, :, lanes]
            d1 = slots[p1, :, lanes] * slots[q1, :, lanes]
            tiles = []
            for j in range(JC):
                t0, t1 = d0[:, 128 * j : 128 * j + 128], d1[:, 128 * j : 128 * j + 128]
                tiles.append(jnp.where(low_lanes, t0, pltpu.roll(t1, 64, 1)))
                tiles.append(jnp.where(low_lanes, pltpu.roll(t0, 64, 1), t1))
            v = along_lanes(jnp.concatenate(tiles, axis=0), wz)
            v = along_rows(rows_to_lanes(v, YC), wr)
            spect[pl.ds(pl.multiple_of(i * (64 * YC), 64 * YC), 64 * YC), :] = lanes_to_rows(v, YC)
            return carry

        def second(i, carry):
            if middle is not None:
                middle(i)
            rows = [pl.ds(i * YC + k, 64, stride=64) for k in range(YC)]
            v = along_rows(jnp.concatenate([spect[r, :] for r in rows], axis=1), wr)
            scale = jnp.concatenate([table[i * YC + k] for k in range(YC)], axis=1)
            v = along_rows(v * scale, wr)
            for k in range(YC):
                spect[rows[k], :] = v[:, 128 * k : 128 * k + 128]
            return carry

        def third(i, carry):
            v = spect[pl.ds(pl.multiple_of(i * (64 * YC), 64 * YC), 64 * YC), :]
            v = along_rows(rows_to_lanes(v, YC), wr)
            v = along_lanes(lanes_to_rows(v, YC), wz)
            v0, v1 = [], []
            for j in range(JC):
                even, odd = v[128 * j : 128 * j + 64], v[128 * j + 64 : 128 * j + 128]
                v0.append(jnp.where(low_lanes, even, pltpu.roll(odd, 64, 1)))
                v1.append(jnp.where(low_lanes, pltpu.roll(even, 64, 1), odd))
            update(lanes_of(i), jnp.concatenate(v0, axis=1), jnp.concatenate(v1, axis=1))
            if after is not None:
                after(i)
            return carry

        lax.fori_loop(0, 64 // YC, first, 0)
        lax.fori_loop(0, 64 // YC, second, 0)
        lax.fori_loop(0, 64 // YC, third, 0)

    def keep_at(i, j):
        return keep_ref[i, j].astype(F32)

    self_keep = keep_at(at.band, at.band)

    def self_update(lanes, v0, v1):
        orbital = slots[0, :, lanes]
        for s in range(4):
            rows = slice(16 * s, 16 * s + 16)
            mine = self_keep * (2 * l + c == s).astype(F32)
            acc[0, s % 2, s // 2, :, lanes] = (mine * v0[rows]) * orbital[rows]

    def pair_batch(b, before, middle, after):
        pairs, scales = [], []
        for k in range(2):
            entries = {(pl_, pc_): PAIRS[pl_][pc_][b][k] for pl_ in (0, 1) for pc_ in (0, 1)}

            def value(field):
                return pick({key: field(entry) for key, entry in entries.items()})

            bits = (at.z // 2, at.y // 2, at.h)
            phase = sum(value(lambda t: t[4] >> n & 1) * bits[n] for n in range(3)) % 2
            unused = sum(value(lambda t: t[5] >> n & 1) * bits[n] for n in range(3)) % 2

            def both(field):
                v0 = value(lambda t: field(t, 0))
                return v0 + phase * (value(lambda t: field(t, 1)) - v0)

            p = both(lambda t, w: t[2 * w])
            q = both(lambda t, w: t[2 * w + 1])

            def band_of(which):
                def part(axis):
                    def get(host_l, t, w):
                        index = t[2 * w + which]
                        if index == 0:
                            return 0
                        element = ELEMENTS[host_l][index - 1]
                        return element[1 if (element[2] and w == 1) else 0][axis]

                    def table_of(w):
                        return pick({key: get(key[0], entry, w) for key, entry in entries.items()})

                    v0 = table_of(0)
                    return v0 + phase * (table_of(1) - v0)

                z = (at.z + part(0)) % 4
                y = (at.y + part(1)) % 4
                h = (at.h + part(2)) % 2
                return (z * 4 + y) * 2 + h

            weight = keep_at(band_of(0), band_of(1))
            pairs.append((p, q))
            scales.append(weight * (jnp.int32(1) - unused).astype(F32))

        def update(lanes, v0, v1):
            for (p, q), scale, v in zip(pairs, scales, (v0, v1)):
                scaled = scale * v
                to_p = scaled * slots[q, :, lanes]
                to_q = scaled * slots[p, :, lanes]
                for target, term in ((p, to_p), (q, to_q)):
                    for s in range(4):
                        acc[target, s % 2, s // 2, :, lanes] += term[16 * s : 16 * s + 16]

        transform(pairs, update, before, middle, after)

    def exchange(e, lanes, i=0):
        return pltpu.make_async_remote_copy(
            src_ref=acc.at[e, 1 - c, :, :, lanes], dst_ref=xbuf.at[e, :, :, lanes],
            send_sem=x_send.at[e], recv_sem=x_recv.at[e * 4 + i],
            device_id=sibling, device_id_type=MESH)

    def send_back(move, lanes, i=0):
        return pltpu.make_async_remote_copy(
            src_ref=acc.at[move.e + 1, c, :, :, lanes],
            dst_ref=rbuf.at[move.l * K + move.e, :, :, lanes],
            send_sem=r_send.at[move.e], recv_sem=r_recv.at[(move.l * K + move.e) * 4 + i],
            device_id=parent(move), device_id_type=MESH)

    def swap(lanes, i=0):
        return pltpu.make_async_remote_copy(
            src_ref=acc.at[0, c, 1 - l, :, lanes], dst_ref=fbuf.at[:, lanes],
            send_sem=s_send.at[0], recv_sem=s_recv.at[i], device_id=twin, device_id_type=MESH)

    def start_return(chosen, i):
        for_chip(chosen, lambda chip, e: exchange(e + 1, chunk(i), i).start())

    def collect(move, e, lanes, i):
        send_back(move, lanes, i).wait_recv()
        acc[e, c, :, :, lanes] += rbuf[move.l * K + move.e, :, :, lanes]

    def finish_return(chosen, i):
        lanes = chunk(i)

        def one(chip, e):
            exchange(e + 1, lanes, i).wait_recv()
            acc[e + 1, c, :, :, lanes] += xbuf[e + 1, :, :, lanes]
            for move in moves:
                if (move.from_l, move.slot) == (chip, e + 1):
                    collect(move, e + 1, lanes, i)
            for move in moves:
                if (move.l, move.e) == (chip, e):

                    @pl.when(move.mine)
                    def _():
                        send_back(move, lanes, i).start()

        for_chip(chosen, one)

    def at_step(i, step, *actions):
        @pl.when(i == step)
        def _():
            for action, *arguments in actions:
                action(*arguments)

    def first_before(i):
        at_step(i, 1, (pass_on, EARLY_FAR, 1))
        at_step(i, 2, (pass_on, EARLY_NEAR, 3), (pass_on, EARLY_FAR, 2))
        at_step(i, 3, (pass_on, EARLY_FAR, 3))
        passed_on(EARLY_NEAR, i)
        passed_on(EARLY_FAR, i)

    def first_middle(i):
        at_step(i, 0, (pass_on, LATE_NEAR, 0))

    def first_after(i):
        start_return(BACK_EARLY, i)
        start_return(BACK_EARLY_JOIN, i)

        @pl.when(i > 1)
        def _():
            finish_return(BACK_EARLY, i - 2)

        @pl.when(i > 0)
        def _():
            pass_on(LATE_NEAR, i)

    def second_before(i):
        at_step(i, 1, (finish_return, BACK_EARLY, 3))
        pass_on(LATE_FAR, i)
        passed_on(LATE_NEAR, i)
        passed_on(LATE_FAR, i)

    def second_after(i):
        start_return(BACK_LATE, i)
        start_return(BACK_LATE_JOIN, i)
        exchange(0, chunk(i), i).start()
        finish_return(BACK_EARLY_JOIN, i)

        @pl.when(i > 1)
        def _():
            finish_return(BACK_LATE, i - 2)

    table_copy.wait()
    transform([(0, 0), (0, 0)], self_update)
    pass_on(EARLY_NEAR, 0)
    pass_on(EARLY_NEAR, 1)
    pass_on(EARLY_FAR, 0)
    pass_on(EARLY_NEAR, 2)
    pair_batch(0, first_before, first_middle, first_after)
    finish_return(BACK_EARLY, 2)
    pair_batch(1, second_before, None, second_after)
    finish_return(BACK_LATE, 2)
    finish_return(BACK_LATE, 3)

    def gather(i, carry):
        lanes = chunk(i)
        finish_return(BACK_LATE_JOIN, i)
        exchange(0, lanes, i).wait_recv()
        acc[0, c, :, :, lanes] += xbuf[0, :, :, lanes]
        for move in moves:
            if move.slot == 0:

                @pl.when(move.here)
                def _():
                    collect(move, 0, lanes, i)

        swap(lanes, i).start()
        return carry

    def finish(i, carry):
        lanes = chunk(i)
        swap(lanes, i).wait_recv()
        out_ref[:, lanes] = acc[0, c, l, :, lanes] + fbuf[:, lanes]
        return carry

    lax.fori_loop(0, 4, gather, 0)
    lax.fori_loop(0, 4, finish, 0)

    swap(everything).wait_send()
    exchange(0, everything).wait_send()
    elements = [range(len(ELEMENTS[0])), range(len(ELEMENTS[1]))]
    for_chip(elements, lambda chip, e: forward(e, everything).wait_send())
    for_chip(elements, lambda chip, e: exchange(e + 1, everything).wait_send())
    for move in moves:

        @pl.when(move.here)
        def _():
            orbital_out(move, everything).wait_send()

        @pl.when(move.mine)
        def _():
            send_back(move, everything).wait_send()


def body(orbitals, pair_keep, wz, wr, table):
    dma = pltpu.SemaphoreType.DMA
    out = pl.pallas_call(
        kernel,
        name="exchange",
        out_shape=jax.ShapeDtypeStruct((16, NYZ), F32),
        in_specs=[
            pl.BlockSpec(memory_space=pl.ANY),
            pl.BlockSpec(memory_space=pltpu.SMEM),
            pl.BlockSpec(memory_space=pltpu.VMEM),
            pl.BlockSpec(memory_space=pltpu.VMEM),
            pl.BlockSpec(memory_space=pl.ANY),
        ],
        out_specs=pl.BlockSpec(memory_space=pltpu.VMEM),
        scratch_shapes=[
            pltpu.VMEM((K + 1, NX, NYZ), F32),
            pltpu.VMEM((K + 1, 2, 2, 16, NYZ), F32),
            pltpu.VMEM((K + 1, 2, 16, NYZ), F32),
            pltpu.VMEM((2 * K, 2, 16, NYZ), F32),
            pltpu.VMEM((16, NYZ), F32),
            pltpu.VMEM((64 * 64, 128), F32),
            pltpu.VMEM((64, 64, 128), F32),
            dma((2,)),
            dma((2 * K,)), dma((4 * K,)),
            dma((K,)), dma((4 * K,)),
            dma((K + 1,)), dma((4 * K + 4,)),
            dma((K,)), dma((8 * K,)),
            dma((1,)), dma((4,)),
        ],
        compiler_params=pltpu.CompilerParams(
            collective_id=0, has_side_effects=True, vmem_limit_bytes=56 << 20),
    )(orbitals.reshape(NX, NYZ), pair_keep, wz, wr, table)
    return out.reshape(1, 16, NYZ)


def solution(mesh):
    constants = (lane_matrix(), sublane_matrix(), screened_table())

    def call(orbitals, pair_keep):
        return body(orbitals, pair_keep, *[jnp.asarray(x) for x in constants])

    return jax.shard_map(
        call,
        mesh=mesh,
        in_specs=(P("band", None, None), P()),
        out_specs=P("band", "pair", None),
        check_vma=False,
    )
```

```python
import functools
import math

import jax
import jax.numpy as jnp
import ml_dtypes
import numpy as np
from jax import lax
from jax.experimental import pallas as pl
from jax.experimental.pallas import tpu as pltpu
from jax.sharding import PartitionSpec as P

NX = NY = NZ = 64
NYZ = NY * NZ
CELL_LENGTH = 46.92
SCREEN_OMEGA = 0.11
BF16 = jnp.bfloat16
F32 = jnp.float32
MESH = pl.DeviceIdType.MESH

ELEMENTS = [[((0, 2, 0), (0, 2, 0), 0, None), ((2, 0, 1), (2, 0, 0), 1, None), ((3, 1, 0), (3, 1, 0), 0, ((0, 0, 0), 1, 3)), ((3, 0, 0), (3, 0, 0), 0, None), ((0, 0, 1), (0, 0, 1), 0, None)], [((0, 3, 0), (0, 3, 0), 0, None), ((1, 0, 1), (1, 0, 1), 0, None), ((3, 1, 0), (3, 1, 0), 0, None), ((0, 2, 0), (0, 2, 0), 0, ((0, 0, 0), 0, 1)), ((0, 0, 1), (0, 0, 1), 0, None), ((1, 0, 0), (1, 0, 0), 0, None)]]
EARLY_NEAR = [[0, 1], [0, 1, 2]]
EARLY_FAR = [[2], [3]]
LATE_NEAR = [[3, 4], [4, 5]]
LATE_FAR = [[], []]
BACK_EARLY = [[1, 2], [1, 3]]
BACK_EARLY_JOIN = [[], []]
BACK_LATE = [[0, 3, 4], [0, 2, 4, 5]]
BACK_LATE_JOIN = [[], []]
PAIRS = [[[[(3, 1, 3, 1, 0, 0), (1, 2, 1, 2, 1, 0)], [(4, 5, 4, 5, 0, 0), (1, 0, 1, 5, 3, 0)]], [[(3, 0, 3, 0, 0, 0), (0, 2, 0, 2, 1, 0)], [(4, 1, 4, 1, 0, 0), (5, 0, 5, 0, 0, 4)]]], [[[(1, 2, 1, 2, 0, 0), (2, 3, 2, 3, 0, 0)], [(1, 5, 1, 5, 0, 0), (0, 6, 0, 6, 0, 0)]], [[(1, 0, 1, 0, 0, 0), (4, 2, 4, 2, 0, 0)], [(3, 5, 3, 5, 0, 0), (6, 3, 6, 3, 0, 0)]]]]
K = max(len(ELEMENTS[0]), len(ELEMENTS[1]))
JC = 8
YC = 2 * JC
CHUNK = 128 * JC


def cas_matrix():
    counter = np.arange(64)
    angles = 2.0 * math.pi * (np.outer(counter, counter) % 64) / 64
    return np.cos(angles) + np.sin(angles)


def split_constant(matrix):
    high = matrix.astype(ml_dtypes.bfloat16)
    low = (matrix - high.astype(np.float64)).astype(ml_dtypes.bfloat16)
    return high, low


def lane_matrix():
    high, low = split_constant(np.kron(np.eye(2), cas_matrix()))
    row = np.concatenate([high, low], axis=1)
    return np.concatenate([row, row], axis=0)


def sublane_matrix():
    high, low = split_constant(cas_matrix())
    return np.concatenate([np.concatenate([high, high], 1), np.concatenate([low, low], 1)], 0)


def screened_table():
    counter = np.arange(64)
    wave = np.minimum(counter, 64 - counter) * (2.0 * math.pi / CELL_LENGTH)
    square = wave[:, None, None] ** 2 + wave[None, :, None] ** 2 + wave[None, None, :] ** 2
    guarded = np.where(square > 0.0, square, 1.0)
    screened = 4.0 * math.pi / guarded * -np.expm1(-guarded / (4.0 * SCREEN_OMEGA**2))
    table = np.where(square > 0.0, screened, 0.0) * (-1.0 / (NX * NY * NZ))
    return np.concatenate([table, table], axis=2).astype(np.float32)


def dot(a, b):
    return jnp.dot(a, b, preferred_element_type=F32)


def halves(v):
    high = v.astype(BF16)
    low = (v - high.astype(F32)).astype(BF16)
    return high, low


def along_lanes(v, weights):
    out = dot(jnp.concatenate(halves(v), axis=1), weights)
    return out[:, :128] + out[:, 128:]


def along_rows(v, weights):
    out = dot(weights, jnp.concatenate(halves(v), axis=0))
    return out[:64] + out[64:]


def rows_to_lanes(v, count):
    return jnp.concatenate([v[64 * i : 64 * i + 64] for i in range(count)], axis=1)


def lanes_to_rows(v, count):
    return jnp.concatenate([v[:, 128 * i : 128 * i + 128] for i in range(count)], axis=0)


class Place:
    def __init__(self):
        band = lax.axis_index("band")
        pair = lax.axis_index("pair")
        self.z, self.y, self.h = band // 8, (band // 2) % 4, band % 2
        self.l, self.c = pair // 2, pair % 2
        self.band = band

    def shifted(self, u, sign):
        z = (self.z + 4 + sign * u[0]) % 4
        y = (self.y + 4 + sign * u[1]) % 4
        h = (self.h + u[2]) % 2
        return z, y, h

    def band_at(self, u, sign):
        z, y, h = self.shifted(u, sign)
        return (z * 4 + y) * 2 + h

    def phase_at(self, mask, u, sign):
        z, y, h = self.shifted(u, sign)
        bits = (z // 2, y // 2, h)
        return sum(bit for k, bit in enumerate(bits) if mask >> k & 1) % 2


class Transfer:
    def __init__(self, place, l, e, step, from_l, slot, mask=0, value=0):
        self.l, self.e, self.step, self.from_l, self.slot = l, e, step, from_l, slot
        self.here, self.mine = place.l == from_l, place.l == l
        if mask:
            self.here = self.here & (place.phase_at(mask, step, -1) == value)
            self.mine = self.mine & (place.phase_at(mask, (0, 0, 0), 1) == value)


def transfers(place):
    found = []
    for l in (0, 1):
        for e, (first, second, mask, relay) in enumerate(ELEMENTS[l]):
            if relay is not None:
                found.append(Transfer(place, l, e, *relay))
                continue
            for value, u in enumerate((first, second) if mask else (first,)):
                from_l = l if u[2] == 0 else 1 - l
                found.append(Transfer(place, l, e, u, from_l, 0, mask, value))
    return found


def kernel(orb_ref, keep_ref, wz_ref, wr_ref, table_hbm, out_ref,
           slots, acc, xbuf, rbuf, fbuf, spect, table,
           local_sem, d_send, d_recv, f_send, f_recv, x_send, x_recv, r_send, r_recv, s_send, s_recv):
    at = Place()
    l, c = at.l, at.c
    sibling = (at.band, 2 * l + 1 - c)
    twin = (at.band, 2 * (1 - l) + c)

    def pick(values):
        out = 0
        for (pl_, pc_), value in values.items():
            if value != 0:
                out = out + value * ((l == pl_) & (c == pc_)).astype(jnp.int32)
        return out

    own_copy = pltpu.make_async_copy(orb_ref, slots.at[0], local_sem.at[0])
    own_copy.start()
    table_copy = pltpu.make_async_copy(table_hbm, table, local_sem.at[1])
    table_copy.start()

    barrier = pltpu.get_barrier_semaphore()
    peers = 2
    pl.semaphore_signal(barrier, inc=1, device_id=sibling, device_id_type=MESH)
    pl.semaphore_signal(barrier, inc=1, device_id=twin, device_id_type=MESH)
    moves = transfers(at)

    def child(move):
        return (at.band_at(move.step, -1), 2 * move.l + c)

    def parent(move):
        return (at.band_at(move.step, 1), 2 * move.from_l + c)

    for move in moves:
        peers = peers + move.here.astype(jnp.int32) + move.mine.astype(jnp.int32)

        @pl.when(move.here)
        def _():
            pl.semaphore_signal(barrier, inc=1, device_id=child(move), device_id_type=MESH)

        @pl.when(move.mine)
        def _():
            pl.semaphore_signal(barrier, inc=1, device_id=parent(move), device_id_type=MESH)

    own_copy.wait()
    pl.semaphore_wait(barrier, peers)

    my_rows = pl.ds(pl.multiple_of(32 * c, 32), 32)

    def chunk(i):
        return pl.ds(pl.multiple_of(i * CHUNK, CHUNK), CHUNK)

    everything = pl.ds(0, NYZ)

    def orbital_out(move, lanes, i=0):
        return pltpu.make_async_remote_copy(
            src_ref=slots.at[move.slot, my_rows, lanes],
            dst_ref=slots.at[move.e + 1, my_rows, lanes],
            send_sem=d_send.at[move.l * K + move.e], recv_sem=d_recv.at[move.e * 4 + i],
            device_id=child(move), device_id_type=MESH)

    def is_early(move):
        return move.e in EARLY_NEAR[move.l] or move.e in EARLY_FAR[move.l]

    def set_out(early, i):
        for move in moves:
            if move.slot == 0 and is_early(move) == early:

                @pl.when(move.here)
                def _():
                    orbital_out(move, chunk(i), i).start()

    for i in range(4):
        set_out(True, i)

    for e in range(1, K + 1):
        acc[e] = jnp.zeros(acc.shape[1:], F32)

    def forward(e, lanes, i=0):
        return pltpu.make_async_remote_copy(
            src_ref=slots.at[e + 1, my_rows, lanes], dst_ref=slots.at[e + 1, my_rows, lanes],
            send_sem=f_send.at[e], recv_sem=f_recv.at[e * 4 + i],
            device_id=sibling, device_id_type=MESH)

    def for_chip(chosen, body):
        for chip in (0, 1):
            if chosen[chip]:

                @pl.when(l == chip)
                def _():
                    for e in chosen[chip]:
                        body(chip, e)

    def pass_on(chosen, i):
        def relayed(chip, e):
            return any((move.from_l, move.slot) == (chip, e + 1) for move in moves)

        chosen = [sorted(chosen[chip], key=lambda e: not relayed(chip, e)) for chip in (0, 1)]

        def one(chip, e):
            arriving = [move for move in moves if (move.l, move.e) == (chip, e)][0]
            orbital_out(arriving, chunk(i), i).wait_recv()
            forward(e, chunk(i), i).start()
            for move in moves:
                if (move.from_l, move.slot) == (chip, e + 1):
                    orbital_out(move, chunk(i), i).start()

        for_chip(chosen, one)

    def passed_on(chosen, i):
        for_chip(chosen, lambda chip, e: forward(e, chunk(i), i).wait_recv())

    low_lanes = lax.broadcasted_iota(jnp.int32, (64, 128), 1) < 64

    def lanes_of(i):
        return chunk(i)

    def transform(pairs, update, before=None, middle=None, after=None):
        wz, wr = wz_ref[...], wr_ref[...]
        (p0, q0), (p1, q1) = pairs

        def first(i, carry):
            if before is not None:
                before(i)
            lanes = lanes_of(i)
            d0 = slots[p0, :, lanes] * slots[q0, :, lanes]
            d1 = slots[p1, :, lanes] * slots[q1, :, lanes]
            tiles = []
            for j in range(JC):
                t0, t1 = d0[:, 128 * j : 128 * j + 128], d1[:, 128 * j : 128 * j + 128]
                tiles.append(jnp.where(low_lanes, t0, pltpu.roll(t1, 64, 1)))
                tiles.append(jnp.where(low_lanes, pltpu.roll(t0, 64, 1), t1))
            v = along_lanes(jnp.concatenate(tiles, axis=0), wz)
            v = along_rows(rows_to_lanes(v, YC), wr)
            spect[pl.ds(pl.multiple_of(i * (64 * YC), 64 * YC), 64 * YC), :] = lanes_to_rows(v, YC)
            return carry

        def second(i, carry):
            if middle is not None:
                middle(i)
            rows = [pl.ds(i * YC + k, 64, stride=64) for k in range(YC)]
            v = along_rows(jnp.concatenate([spect[r, :] for r in rows], axis=1), wr)
            scale = jnp.concatenate([table[i * YC + k] for k in range(YC)], axis=1)
            v = along_rows(v * scale, wr)
            for k in range(YC):
                spect[rows[k], :] = v[:, 128 * k : 128 * k + 128]
            return carry

        def third(i, carry):
            v = spect[pl.ds(pl.multiple_of(i * (64 * YC), 64 * YC), 64 * YC), :]
            v = along_rows(rows_to_lanes(v, YC), wr)
            v = along_lanes(lanes_to_rows(v, YC), wz)
            v0, v1 = [], []
            for j in range(JC):
                even, odd = v[128 * j : 128 * j + 64], v[128 * j + 64 : 128 * j + 128]
                v0.append(jnp.where(low_lanes, even, pltpu.roll(odd, 64, 1)))
                v1.append(jnp.where(low_lanes, pltpu.roll(even, 64, 1), odd))
            update(lanes_of(i), jnp.concatenate(v0, axis=1), jnp.concatenate(v1, axis=1))
            if after is not None:
                after(i)
            return carry

        lax.fori_loop(0, 64 // YC, first, 0)
        lax.fori_loop(0, 64 // YC, second, 0, unroll=True)
        lax.fori_loop(0, 64 // YC, third, 0)

    def keep_at(i, j):
        return keep_ref[i, j].astype(F32)

    self_keep = keep_at(at.band, at.band)

    def self_update(lanes, v0, v1):
        orbital = slots[0, :, lanes]
        for s in range(4):
            rows = slice(16 * s, 16 * s + 16)
            mine = self_keep * (2 * l + c == s).astype(F32)
            acc[0, s % 2, s // 2, :, lanes] = (mine * v0[rows]) * orbital[rows]

    def pair_batch(b, before, middle, after):
        pairs, scales = [], []
        for k in range(2):
            entries = {(pl_, pc_): PAIRS[pl_][pc_][b][k] for pl_ in (0, 1) for pc_ in (0, 1)}

            def value(field):
                return pick({key: field(entry) for key, entry in entries.items()})

            bits = (at.z // 2, at.y // 2, at.h)
            phase = sum(value(lambda t: t[4] >> n & 1) * bits[n] for n in range(3)) % 2
            unused = sum(value(lambda t: t[5] >> n & 1) * bits[n] for n in range(3)) % 2

            def both(field):
                v0 = value(lambda t: field(t, 0))
                return v0 + phase * (value(lambda t: field(t, 1)) - v0)

            p = both(lambda t, w: t[2 * w])
            q = both(lambda t, w: t[2 * w + 1])

            def band_of(which):
                def part(axis):
                    def get(host_l, t, w):
                        index = t[2 * w + which]
                        if index == 0:
                            return 0
                        element = ELEMENTS[host_l][index - 1]
                        return element[1 if (element[2] and w == 1) else 0][axis]

                    def table_of(w):
                        return pick({key: get(key[0], entry, w) for key, entry in entries.items()})

                    v0 = table_of(0)
                    return v0 + phase * (table_of(1) - v0)

                z = (at.z + part(0)) % 4
                y = (at.y + part(1)) % 4
                h = (at.h + part(2)) % 2
                return (z * 4 + y) * 2 + h

            weight = keep_at(band_of(0), band_of(1))
            pairs.append((p, q))
            scales.append(weight * (jnp.int32(1) - unused).astype(F32))

        def update(lanes, v0, v1):
            for (p, q), scale, v in zip(pairs, scales, (v0, v1)):
                scaled = scale * v
                to_p = scaled * slots[q, :, lanes]
                to_q = scaled * slots[p, :, lanes]
                for target, term in ((p, to_p), (q, to_q)):
                    for s in range(4):
                        acc[target, s % 2, s // 2, :, lanes] += term[16 * s : 16 * s + 16]

        transform(pairs, update, before, middle, after)

    def exchange(e, lanes, i=0):
        return pltpu.make_async_remote_copy(
            src_ref=acc.at[e, 1 - c, :, :, lanes], dst_ref=xbuf.at[e, :, :, lanes],
            send_sem=x_send.at[e], recv_sem=x_recv.at[e * 4 + i],
            device_id=sibling, device_id_type=MESH)

    def send_back(move, lanes, i=0):
        return pltpu.make_async_remote_copy(
            src_ref=acc.at[move.e + 1, c, :, :, lanes],
            dst_ref=rbuf.at[move.l * K + move.e, :, :, lanes],
            send_sem=r_send.at[move.e], recv_sem=r_recv.at[(move.l * K + move.e) * 4 + i],
            device_id=parent(move), device_id_type=MESH)

    def swap(lanes, i=0):
        return pltpu.make_async_remote_copy(
            src_ref=acc.at[0, c, 1 - l, :, lanes], dst_ref=fbuf.at[:, lanes],
            send_sem=s_send.at[0], recv_sem=s_recv.at[i], device_id=twin, device_id_type=MESH)

    def start_return(chosen, i):
        for_chip(chosen, lambda chip, e: exchange(e + 1, chunk(i), i).start())

    def collect(move, e, lanes, i):
        send_back(move, lanes, i).wait_recv()
        acc[e, c, :, :, lanes] += rbuf[move.l * K + move.e, :, :, lanes]

    def finish_return(chosen, i):
        lanes = chunk(i)

        def one(chip, e):
            exchange(e + 1, lanes, i).wait_recv()
            acc[e + 1, c, :, :, lanes] += xbuf[e + 1, :, :, lanes]
            for move in moves:
                if (move.from_l, move.slot) == (chip, e + 1):
                    collect(move, e + 1, lanes, i)
            for move in moves:
                if (move.l, move.e) == (chip, e):

                    @pl.when(move.mine)
                    def _():
                        send_back(move, lanes, i).start()

        for_chip(chosen, one)

    def at_step(i, step, *actions):
        @pl.when(i == step)
        def _():
            for action, *arguments in actions:
                action(*arguments)

    def self_after(i):
        at_step(i, 3, *[(set_out, False, k) for k in range(4)])
        at_step(i, 2, (pass_on, EARLY_NEAR, 0))

    def first_before(i):
        for k in (1, 2, 3):
            at_step(i, k, (pass_on, EARLY_FAR, k))
        passed_on(EARLY_NEAR, i)
        passed_on(EARLY_FAR, i)

    def first_middle(i):
        at_step(i, 0, (pass_on, LATE_NEAR, 0))

    def first_after(i):
        start_return(BACK_EARLY, i)
        start_return(BACK_EARLY_JOIN, i)

        @pl.when(i > 1)
        def _():
            finish_return(BACK_EARLY, i - 2)

        @pl.when(i > 0)
        def _():
            pass_on(LATE_NEAR, i)

    def second_before(i):
        at_step(i, 1, (finish_return, BACK_EARLY, 3))
        pass_on(LATE_FAR, i)
        passed_on(LATE_NEAR, i)
        passed_on(LATE_FAR, i)

    def second_after(i):
        start_return(BACK_LATE, i)
        start_return(BACK_LATE_JOIN, i)
        exchange(0, chunk(i), i).start()
        finish_return(BACK_EARLY_JOIN, i)

        @pl.when(i > 1)
        def _():
            finish_return(BACK_LATE, i - 2)

    table_copy.wait()
    transform([(0, 0), (0, 0)], self_update, after=self_after)
    for i in range(1, 4):
        pass_on(EARLY_NEAR, i)
    pass_on(EARLY_FAR, 0)
    pair_batch(0, first_before, first_middle, first_after)
    finish_return(BACK_EARLY, 2)
    pair_batch(1, second_before, None, second_after)
    finish_return(BACK_LATE, 2)
    finish_return(BACK_LATE, 3)

    def gather(i, carry):
        lanes = chunk(i)
        finish_return(BACK_LATE_JOIN, i)
        exchange(0, lanes, i).wait_recv()
        acc[0, c, :, :, lanes] += xbuf[0, :, :, lanes]
        for move in moves:
            if move.slot == 0:

                @pl.when(move.here)
                def _():
                    collect(move, 0, lanes, i)

        swap(lanes, i).start()
        return carry

    def finish(i, carry):
        lanes = chunk(i)
        swap(lanes, i).wait_recv()
        out_ref[:, lanes] = acc[0, c, l, :, lanes] + fbuf[:, lanes]
        return carry

    lax.fori_loop(0, 4, gather, 0)
    lax.fori_loop(0, 4, finish, 0)

    swap(everything).wait_send()
    exchange(0, everything).wait_send()
    elements = [range(len(ELEMENTS[0])), range(len(ELEMENTS[1]))]
    for_chip(elements, lambda chip, e: forward(e, everything).wait_send())
    for_chip(elements, lambda chip, e: exchange(e + 1, everything).wait_send())
    for move in moves:

        @pl.when(move.here)
        def _():
            orbital_out(move, everything).wait_send()

        @pl.when(move.mine)
        def _():
            send_back(move, everything).wait_send()


def body(orbitals, pair_keep, wz, wr, table):
    dma = pltpu.SemaphoreType.DMA
    out = pl.pallas_call(
        kernel,
        name="exchange",
        out_shape=jax.ShapeDtypeStruct((16, NYZ), F32),
        in_specs=[
            pl.BlockSpec(memory_space=pl.ANY),
            pl.BlockSpec(memory_space=pltpu.SMEM),
            pl.BlockSpec(memory_space=pltpu.VMEM),
            pl.BlockSpec(memory_space=pltpu.VMEM),
            pl.BlockSpec(memory_space=pl.ANY),
        ],
        out_specs=pl.BlockSpec(memory_space=pltpu.VMEM),
        scratch_shapes=[
            pltpu.VMEM((K + 1, NX, NYZ), F32),
            pltpu.VMEM((K + 1, 2, 2, 16, NYZ), F32),
            pltpu.VMEM((K + 1, 2, 16, NYZ), F32),
            pltpu.VMEM((2 * K, 2, 16, NYZ), F32),
            pltpu.VMEM((16, NYZ), F32),
            pltpu.VMEM((64 * 64, 128), F32),
            pltpu.VMEM((64, 64, 128), F32),
            dma((2,)),
            dma((2 * K,)), dma((4 * K,)),
            dma((K,)), dma((4 * K,)),
            dma((K + 1,)), dma((4 * K + 4,)),
            dma((K,)), dma((8 * K,)),
            dma((1,)), dma((4,)),
        ],
        compiler_params=pltpu.CompilerParams(
            collective_id=0, has_side_effects=True, vmem_limit_bytes=56 << 20),
    )(orbitals.reshape(NX, NYZ), pair_keep, wz, wr, table)
    return out.reshape(1, 16, NYZ)


def solution(mesh):
    constants = (lane_matrix(), sublane_matrix(), screened_table())

    def call(orbitals, pair_keep):
        return body(orbitals, pair_keep, *[jnp.asarray(x) for x in constants])

    return jax.shard_map(
        call,
        mesh=mesh,
        in_specs=(P("band", None, None), P()),
        out_specs=P("band", "pair", None),
        check_vma=False,
    )
```

```python
import functools
import math

import jax
import jax.numpy as jnp
import ml_dtypes
import numpy as np
from jax import lax
from jax.experimental import pallas as pl
from jax.experimental.pallas import tpu as pltpu
from jax.sharding import PartitionSpec as P

NX = NY = NZ = 64
NYZ = NY * NZ
CELL_LENGTH = 46.92
SCREEN_OMEGA = 0.11
BF16 = jnp.bfloat16
F32 = jnp.float32
MESH = pl.DeviceIdType.MESH

ELEMENTS = [[((0, 2, 0), (0, 2, 0), 0, None), ((2, 0, 1), (2, 0, 0), 1, None), ((3, 1, 0), (3, 1, 0), 0, ((0, 0, 0), 1, 3)), ((3, 0, 0), (3, 0, 0), 0, None), ((0, 0, 1), (0, 0, 1), 0, None)], [((0, 3, 0), (0, 3, 0), 0, None), ((1, 0, 1), (1, 0, 1), 0, None), ((3, 1, 0), (3, 1, 0), 0, None), ((0, 2, 0), (0, 2, 0), 0, ((0, 0, 0), 0, 1)), ((0, 0, 1), (0, 0, 1), 0, None), ((1, 0, 0), (1, 0, 0), 0, None)]]
EARLY_NEAR = [[0, 1], [0, 1, 2]]
EARLY_FAR = [[2], [3]]
LATE_NEAR = [[3, 4], [4, 5]]
LATE_FAR = [[], []]
BACK_EARLY = [[1, 2], [1, 3]]
BACK_EARLY_JOIN = [[], []]
BACK_LATE = [[0, 3, 4], [0, 2, 4, 5]]
BACK_LATE_JOIN = [[], []]
PAIRS = [[[[(3, 1, 3, 1, 0, 0), (1, 2, 1, 2, 1, 0)], [(4, 5, 4, 5, 0, 0), (1, 0, 1, 5, 3, 0)]], [[(3, 0, 3, 0, 0, 0), (0, 2, 0, 2, 1, 0)], [(4, 1, 4, 1, 0, 0), (5, 0, 5, 0, 0, 4)]]], [[[(1, 2, 1, 2, 0, 0), (2, 3, 2, 3, 0, 0)], [(1, 5, 1, 5, 0, 0), (0, 6, 0, 6, 0, 0)]], [[(1, 0, 1, 0, 0, 0), (4, 2, 4, 2, 0, 0)], [(3, 5, 3, 5, 0, 0), (6, 3, 6, 3, 0, 0)]]]]
K = max(len(ELEMENTS[0]), len(ELEMENTS[1]))
JC = 8
YC = 2 * JC
CHUNK = 128 * JC


def cas_matrix():
    counter = np.arange(64)
    angles = 2.0 * math.pi * (np.outer(counter, counter) % 64) / 64
    return np.cos(angles) + np.sin(angles)


def split_constant(matrix):
    high = matrix.astype(ml_dtypes.bfloat16)
    low = (matrix - high.astype(np.float64)).astype(ml_dtypes.bfloat16)
    return high, low


def lane_matrix():
    high, low = split_constant(np.kron(np.eye(2), cas_matrix()))
    row = np.concatenate([high, low], axis=1)
    return np.concatenate([row, row], axis=0)


def sublane_matrix():
    high, low = split_constant(cas_matrix())
    return np.concatenate([np.concatenate([high, high], 1), np.concatenate([low, low], 1)], 0)


def screened_table():
    counter = np.arange(64)
    wave = np.minimum(counter, 64 - counter) * (2.0 * math.pi / CELL_LENGTH)
    square = wave[:, None, None] ** 2 + wave[None, :, None] ** 2 + wave[None, None, :] ** 2
    guarded = np.where(square > 0.0, square, 1.0)
    screened = 4.0 * math.pi / guarded * -np.expm1(-guarded / (4.0 * SCREEN_OMEGA**2))
    table = np.where(square > 0.0, screened, 0.0) * (-1.0 / (NX * NY * NZ))
    return np.concatenate([table, table], axis=2).astype(np.float32)


def dot(a, b):
    return jnp.dot(a, b, preferred_element_type=F32)


def halves(v):
    high = v.astype(BF16)
    low = (v - high.astype(F32)).astype(BF16)
    return high, low


def along_lanes(v, weights):
    out = dot(jnp.concatenate(halves(v), axis=1), weights)
    return out[:, :128] + out[:, 128:]


def along_rows(v, weights):
    out = dot(weights, jnp.concatenate(halves(v), axis=0))
    return out[:64] + out[64:]


def rows_to_lanes(v, count):
    return jnp.concatenate([v[64 * i : 64 * i + 64] for i in range(count)], axis=1)


def lanes_to_rows(v, count):
    return jnp.concatenate([v[:, 128 * i : 128 * i + 128] for i in range(count)], axis=0)


class Place:
    def __init__(self):
        band = lax.axis_index("band")
        pair = lax.axis_index("pair")
        self.z, self.y, self.h = band // 8, (band // 2) % 4, band % 2
        self.l, self.c = pair // 2, pair % 2
        self.band = band

    def shifted(self, u, sign):
        z = (self.z + 4 + sign * u[0]) % 4
        y = (self.y + 4 + sign * u[1]) % 4
        h = (self.h + u[2]) % 2
        return z, y, h

    def band_at(self, u, sign):
        z, y, h = self.shifted(u, sign)
        return (z * 4 + y) * 2 + h

    def phase_at(self, mask, u, sign):
        z, y, h = self.shifted(u, sign)
        bits = (z // 2, y // 2, h)
        return sum(bit for k, bit in enumerate(bits) if mask >> k & 1) % 2


class Transfer:
    def __init__(self, place, l, e, step, from_l, slot, mask=0, value=0):
        self.l, self.e, self.step, self.from_l, self.slot = l, e, step, from_l, slot
        self.here, self.mine = place.l == from_l, place.l == l
        if mask:
            self.here = self.here & (place.phase_at(mask, step, -1) == value)
            self.mine = self.mine & (place.phase_at(mask, (0, 0, 0), 1) == value)


def transfers(place):
    found = []
    for l in (0, 1):
        for e, (first, second, mask, relay) in enumerate(ELEMENTS[l]):
            if relay is not None:
                found.append(Transfer(place, l, e, *relay))
                continue
            for value, u in enumerate((first, second) if mask else (first,)):
                from_l = l if u[2] == 0 else 1 - l
                found.append(Transfer(place, l, e, u, from_l, 0, mask, value))
    return found


def kernel(orb_ref, keep_ref, wz_ref, wr_ref, table_hbm, out_ref,
           slots, acc, xbuf, rbuf, fbuf, spect, table,
           local_sem, d_send, d_recv, f_send, f_recv, x_send, x_recv, r_send, r_recv, s_send, s_recv):
    at = Place()
    l, c = at.l, at.c
    sibling = (at.band, 2 * l + 1 - c)
    twin = (at.band, 2 * (1 - l) + c)

    def pick(values):
        out = 0
        for (pl_, pc_), value in values.items():
            if value != 0:
                out = out + value * ((l == pl_) & (c == pc_)).astype(jnp.int32)
        return out

    own_copy = pltpu.make_async_copy(orb_ref, slots.at[0], local_sem.at[0])
    own_copy.start()
    table_copy = pltpu.make_async_copy(table_hbm, table, local_sem.at[1])
    table_copy.start()

    barrier = pltpu.get_barrier_semaphore()
    peers = 2
    pl.semaphore_signal(barrier, inc=1, device_id=sibling, device_id_type=MESH)
    pl.semaphore_signal(barrier, inc=1, device_id=twin, device_id_type=MESH)
    moves = transfers(at)

    def child(move):
        return (at.band_at(move.step, -1), 2 * move.l + c)

    def parent(move):
        return (at.band_at(move.step, 1), 2 * move.from_l + c)

    for move in moves:
        peers = peers + move.here.astype(jnp.int32) + move.mine.astype(jnp.int32)

        @pl.when(move.here)
        def _():
            pl.semaphore_signal(barrier, inc=1, device_id=child(move), device_id_type=MESH)

        @pl.when(move.mine)
        def _():
            pl.semaphore_signal(barrier, inc=1, device_id=parent(move), device_id_type=MESH)

    own_copy.wait()
    pl.semaphore_wait(barrier, peers)

    my_rows = pl.ds(pl.multiple_of(32 * c, 32), 32)

    def chunk(i):
        return pl.ds(pl.multiple_of(i * CHUNK, CHUNK), CHUNK)

    everything = pl.ds(0, NYZ)

    def orbital_out(move, lanes, i=0):
        return pltpu.make_async_remote_copy(
            src_ref=slots.at[move.slot, my_rows, lanes],
            dst_ref=slots.at[move.e + 1, my_rows, lanes],
            send_sem=d_send.at[move.l * K + move.e], recv_sem=d_recv.at[move.e * 4 + i],
            device_id=child(move), device_id_type=MESH)

    def is_early(move):
        return move.e in EARLY_NEAR[move.l] or move.e in EARLY_FAR[move.l]

    def set_out(early, i):
        for move in moves:
            if move.slot == 0 and is_early(move) == early:

                @pl.when(move.here)
                def _():
                    orbital_out(move, chunk(i), i).start()

    for i in range(4):
        set_out(True, i)

    for e in range(1, K + 1):
        acc[e] = jnp.zeros(acc.shape[1:], F32)

    def forward(e, lanes, i=0):
        return pltpu.make_async_remote_copy(
            src_ref=slots.at[e + 1, my_rows, lanes], dst_ref=slots.at[e + 1, my_rows, lanes],
            send_sem=f_send.at[e], recv_sem=f_recv.at[e * 4 + i],
            device_id=sibling, device_id_type=MESH)

    def for_chip(chosen, body):
        for chip in (0, 1):
            if chosen[chip]:

                @pl.when(l == chip)
                def _():
                    for e in chosen[chip]:
                        body(chip, e)

    def pass_on(chosen, i):
        def relayed(chip, e):
            return any((move.from_l, move.slot) == (chip, e + 1) for move in moves)

        chosen = [sorted(chosen[chip], key=lambda e: not relayed(chip, e)) for chip in (0, 1)]

        def one(chip, e):
            arriving = [move for move in moves if (move.l, move.e) == (chip, e)][0]
            orbital_out(arriving, chunk(i), i).wait_recv()
            forward(e, chunk(i), i).start()
            for move in moves:
                if (move.from_l, move.slot) == (chip, e + 1):
                    orbital_out(move, chunk(i), i).start()

        for_chip(chosen, one)

    def passed_on(chosen, i):
        for_chip(chosen, lambda chip, e: forward(e, chunk(i), i).wait_recv())

    low_lanes = lax.broadcasted_iota(jnp.int32, (64, 128), 1) < 64

    def lanes_of(i):
        return chunk(i)

    def transform(pairs, update, before=None, middle=None, after=None):
        wz, wr = wz_ref[...], wr_ref[...]
        (p0, q0), (p1, q1) = pairs

        def first(i, carry):
            if before is not None:
                before(i)
            lanes = lanes_of(i)
            d0 = slots[p0, :, lanes] * slots[q0, :, lanes]
            d1 = slots[p1, :, lanes] * slots[q1, :, lanes]
            tiles = []
            for j in range(JC):
                t0, t1 = d0[:, 128 * j : 128 * j + 128], d1[:, 128 * j : 128 * j + 128]
                tiles.append(jnp.where(low_lanes, t0, pltpu.roll(t1, 64, 1)))
                tiles.append(jnp.where(low_lanes, pltpu.roll(t0, 64, 1), t1))
            v = along_lanes(jnp.concatenate(tiles, axis=0), wz)
            v = along_rows(rows_to_lanes(v, YC), wr)
            spect[pl.ds(pl.multiple_of(i * (64 * YC), 64 * YC), 64 * YC), :] = lanes_to_rows(v, YC)
            return carry

        def second(i, carry):
            if middle is not None:
                middle(i)
            rows = [pl.ds(i * YC + k, 64, stride=64) for k in range(YC)]
            v = along_rows(jnp.concatenate([spect[r, :] for r in rows], axis=1), wr)
            scale = jnp.concatenate([table[i * YC + k] for k in range(YC)], axis=1)
            v = along_rows(v * scale, wr)
            for k in range(YC):
                spect[rows[k], :] = v[:, 128 * k : 128 * k + 128]
            return carry

        def third(i, carry):
            v = spect[pl.ds(pl.multiple_of(i * (64 * YC), 64 * YC), 64 * YC), :]
            v = along_rows(rows_to_lanes(v, YC), wr)
            v = along_lanes(lanes_to_rows(v, YC), wz)
            v0, v1 = [], []
            for j in range(JC):
                even, odd = v[128 * j : 128 * j + 64], v[128 * j + 64 : 128 * j + 128]
                v0.append(jnp.where(low_lanes, even, pltpu.roll(odd, 64, 1)))
                v1.append(jnp.where(low_lanes, pltpu.roll(even, 64, 1), odd))
            update(lanes_of(i), jnp.concatenate(v0, axis=1), jnp.concatenate(v1, axis=1))
            if after is not None:
                after(i)
            return carry

        lax.fori_loop(0, 64 // YC, first, 0)
        lax.fori_loop(0, 64 // YC, second, 0, unroll=True)
        lax.fori_loop(0, 64 // YC, third, 0)

    def keep_at(i, j):
        return keep_ref[i, j].astype(F32)

    self_keep = keep_at(at.band, at.band)

    def self_update(lanes, v0, v1):
        orbital = slots[0, :, lanes]
        for s in range(4):
            rows = slice(16 * s, 16 * s + 16)
            mine = self_keep * (2 * l + c == s).astype(F32)
            acc[0, s % 2, s // 2, :, lanes] = (mine * v0[rows]) * orbital[rows]

    def pair_batch(b, before, middle, after):
        pairs, scales = [], []
        for k in range(2):
            entries = {(pl_, pc_): PAIRS[pl_][pc_][b][k] for pl_ in (0, 1) for pc_ in (0, 1)}

            def value(field):
                return pick({key: field(entry) for key, entry in entries.items()})

            bits = (at.z // 2, at.y // 2, at.h)
            phase = sum(value(lambda t: t[4] >> n & 1) * bits[n] for n in range(3)) % 2
            unused = sum(value(lambda t: t[5] >> n & 1) * bits[n] for n in range(3)) % 2

            def both(field):
                v0 = value(lambda t: field(t, 0))
                return v0 + phase * (value(lambda t: field(t, 1)) - v0)

            p = both(lambda t, w: t[2 * w])
            q = both(lambda t, w: t[2 * w + 1])

            def band_of(which):
                def part(axis):
                    def get(host_l, t, w):
                        index = t[2 * w + which]
                        if index == 0:
                            return 0
                        element = ELEMENTS[host_l][index - 1]
                        return element[1 if (element[2] and w == 1) else 0][axis]

                    def table_of(w):
                        return pick({key: get(key[0], entry, w) for key, entry in entries.items()})

                    v0 = table_of(0)
                    return v0 + phase * (table_of(1) - v0)

                z = (at.z + part(0)) % 4
                y = (at.y + part(1)) % 4
                h = (at.h + part(2)) % 2
                return (z * 4 + y) * 2 + h

            weight = keep_at(band_of(0), band_of(1))
            pairs.append((p, q))
            scales.append(weight * (jnp.int32(1) - unused).astype(F32))

        def update(lanes, v0, v1):
            for (p, q), scale, v in zip(pairs, scales, (v0, v1)):
                scaled = scale * v
                to_p = scaled * slots[q, :, lanes]
                to_q = scaled * slots[p, :, lanes]
                for target, term in ((p, to_p), (q, to_q)):
                    for s in range(4):
                        acc[target, s % 2, s // 2, :, lanes] += term[16 * s : 16 * s + 16]

        transform(pairs, update, before, middle, after)

    def exchange(e, lanes, i=0):
        return pltpu.make_async_remote_copy(
            src_ref=acc.at[e, 1 - c, :, :, lanes], dst_ref=xbuf.at[e, :, :, lanes],
            send_sem=x_send.at[e], recv_sem=x_recv.at[e * 4 + i],
            device_id=sibling, device_id_type=MESH)

    def send_back(move, lanes, i=0):
        return pltpu.make_async_remote_copy(
            src_ref=acc.at[move.e + 1, c, :, :, lanes],
            dst_ref=rbuf.at[move.l * K + move.e, :, :, lanes],
            send_sem=r_send.at[move.e], recv_sem=r_recv.at[(move.l * K + move.e) * 4 + i],
            device_id=parent(move), device_id_type=MESH)

    def swap(lanes, i=0):
        return pltpu.make_async_remote_copy(
            src_ref=acc.at[0, c, 1 - l, :, lanes], dst_ref=fbuf.at[:, lanes],
            send_sem=s_send.at[0], recv_sem=s_recv.at[i], device_id=twin, device_id_type=MESH)

    def start_return(chosen, i):
        for_chip(chosen, lambda chip, e: exchange(e + 1, chunk(i), i).start())

    def collect(move, e, lanes, i):
        send_back(move, lanes, i).wait_recv()
        acc[e, c, :, :, lanes] += rbuf[move.l * K + move.e, :, :, lanes]

    def finish_return(chosen, i):
        lanes = chunk(i)

        def one(chip, e):
            exchange(e + 1, lanes, i).wait_recv()
            acc[e + 1, c, :, :, lanes] += xbuf[e + 1, :, :, lanes]
            for move in moves:
                if (move.from_l, move.slot) == (chip, e + 1):
                    collect(move, e + 1, lanes, i)
            for move in moves:
                if (move.l, move.e) == (chip, e):

                    @pl.when(move.mine)
                    def _():
                        send_back(move, lanes, i).start()

        for_chip(chosen, one)

    def at_step(i, step, *actions):
        @pl.when(i == step)
        def _():
            for action, *arguments in actions:
                action(*arguments)

    def self_after(i):
        at_step(i, 3, (pass_on, EARLY_NEAR, 1))
        at_step(i, 3, *[(set_out, False, k) for k in range(4)])
        at_step(i, 0, (pass_on, EARLY_NEAR, 0))

    def first_before(i):
        for k in (1, 2, 3):
            at_step(i, k, (pass_on, EARLY_FAR, k))
        passed_on(EARLY_NEAR, i)
        passed_on(EARLY_FAR, i)

    def first_middle(i):
        at_step(i, 0, (pass_on, LATE_NEAR, 0))

    def first_after(i):
        start_return(BACK_EARLY, i)
        start_return(BACK_EARLY_JOIN, i)

        @pl.when(i > 1)
        def _():
            finish_return(BACK_EARLY, i - 2)

        @pl.when(i > 0)
        def _():
            pass_on(LATE_NEAR, i)

    def second_before(i):
        at_step(i, 1, (finish_return, BACK_EARLY, 3))
        pass_on(LATE_FAR, i)
        passed_on(LATE_NEAR, i)
        passed_on(LATE_FAR, i)

    def second_after(i):
        start_return(BACK_LATE, i)
        start_return(BACK_LATE_JOIN, i)
        exchange(0, chunk(i), i).start()
        finish_return(BACK_EARLY_JOIN, i)

        @pl.when(i > 1)
        def _():
            finish_return(BACK_LATE, i - 2)

    table_copy.wait()
    transform([(0, 0), (0, 0)], self_update, after=self_after)
    for i in range(2, 4):
        pass_on(EARLY_NEAR, i)
    pass_on(EARLY_FAR, 0)
    pair_batch(0, first_before, first_middle, first_after)
    finish_return(BACK_EARLY, 2)
    pair_batch(1, second_before, None, second_after)
    finish_return(BACK_LATE, 2)
    finish_return(BACK_LATE, 3)

    def gather(i, carry):
        lanes = chunk(i)
        finish_return(BACK_LATE_JOIN, i)
        exchange(0, lanes, i).wait_recv()
        acc[0, c, :, :, lanes] += xbuf[0, :, :, lanes]
        for move in moves:
            if move.slot == 0:

                @pl.when(move.here)
                def _():
                    collect(move, 0, lanes, i)

        swap(lanes, i).start()
        return carry

    def finish(i, carry):
        lanes = chunk(i)
        swap(lanes, i).wait_recv()
        out_ref[:, lanes] = acc[0, c, l, :, lanes] + fbuf[:, lanes]
        return carry

    lax.fori_loop(0, 4, gather, 0)
    lax.fori_loop(0, 4, finish, 0)

    swap(everything).wait_send()
    exchange(0, everything).wait_send()
    elements = [range(len(ELEMENTS[0])), range(len(ELEMENTS[1]))]
    for_chip(elements, lambda chip, e: forward(e, everything).wait_send())
    for_chip(elements, lambda chip, e: exchange(e + 1, everything).wait_send())
    for move in moves:

        @pl.when(move.here)
        def _():
            orbital_out(move, everything).wait_send()

        @pl.when(move.mine)
        def _():
            send_back(move, everything).wait_send()


def body(orbitals, pair_keep, wz, wr, table):
    dma = pltpu.SemaphoreType.DMA
    out = pl.pallas_call(
        kernel,
        name="exchange",
        out_shape=jax.ShapeDtypeStruct((16, NYZ), F32),
        in_specs=[
            pl.BlockSpec(memory_space=pl.ANY),
            pl.BlockSpec(memory_space=pltpu.SMEM),
            pl.BlockSpec(memory_space=pltpu.VMEM),
            pl.BlockSpec(memory_space=pltpu.VMEM),
            pl.BlockSpec(memory_space=pl.ANY),
        ],
        out_specs=pl.BlockSpec(memory_space=pltpu.VMEM),
        scratch_shapes=[
            pltpu.VMEM((K + 1, NX, NYZ), F32),
            pltpu.VMEM((K + 1, 2, 2, 16, NYZ), F32),
            pltpu.VMEM((K + 1, 2, 16, NYZ), F32),
            pltpu.VMEM((2 * K, 2, 16, NYZ), F32),
            pltpu.VMEM((16, NYZ), F32),
            pltpu.VMEM((64 * 64, 128), F32),
            pltpu.VMEM((64, 64, 128), F32),
            dma((2,)),
            dma((2 * K,)), dma((4 * K,)),
            dma((K,)), dma((4 * K,)),
            dma((K + 1,)), dma((4 * K + 4,)),
            dma((K,)), dma((8 * K,)),
            dma((1,)), dma((4,)),
        ],
        compiler_params=pltpu.CompilerParams(
            collective_id=0, has_side_effects=True, vmem_limit_bytes=56 << 20),
    )(orbitals.reshape(NX, NYZ), pair_keep, wz, wr, table)
    return out.reshape(1, 16, NYZ)


def solution(mesh):
    constants = (lane_matrix(), sublane_matrix(), screened_table())

    def call(orbitals, pair_keep):
        return body(orbitals, pair_keep, *[jnp.asarray(x) for x in constants])

    return jax.shard_map(
        call,
        mesh=mesh,
        in_specs=(P("band", None, None), P()),
        out_specs=P("band", "pair", None),
        check_vma=False,
    )
```

```python
import functools
import math

import jax
import jax.numpy as jnp
import ml_dtypes
import numpy as np
from jax import lax
from jax.experimental import pallas as pl
from jax.experimental.pallas import tpu as pltpu
from jax.sharding import PartitionSpec as P

NX = NY = NZ = 64
NYZ = NY * NZ
CELL_LENGTH = 46.92
SCREEN_OMEGA = 0.11
BF16 = jnp.bfloat16
F32 = jnp.float32
MESH = pl.DeviceIdType.MESH

ELEMENTS = [[((0, 2, 0), (0, 2, 0), 0, None), ((2, 0, 1), (2, 0, 0), 1, None), ((3, 1, 0), (3, 1, 0), 0, ((0, 0, 0), 1, 3)), ((3, 0, 0), (3, 0, 0), 0, None), ((0, 0, 1), (0, 0, 1), 0, None)], [((0, 3, 0), (0, 3, 0), 0, None), ((1, 0, 1), (1, 0, 1), 0, None), ((3, 1, 0), (3, 1, 0), 0, None), ((0, 2, 0), (0, 2, 0), 0, ((0, 0, 0), 0, 1)), ((0, 0, 1), (0, 0, 1), 0, None), ((1, 0, 0), (1, 0, 0), 0, None)]]
EARLY_NEAR = [[0, 1], [0, 1, 2]]
EARLY_FAR = [[2], [3]]
LATE_NEAR = [[3, 4], [4, 5]]
LATE_FAR = [[], []]
BACK_EARLY = [[1, 2], [1, 3]]
BACK_EARLY_JOIN = [[], []]
BACK_LATE = [[0, 3, 4], [0, 2, 4, 5]]
BACK_LATE_JOIN = [[], []]
PAIRS = [[[[(3, 1, 3, 1, 0, 0), (1, 2, 1, 2, 1, 0)], [(4, 5, 4, 5, 0, 0), (1, 0, 1, 5, 3, 0)]], [[(3, 0, 3, 0, 0, 0), (0, 2, 0, 2, 1, 0)], [(4, 1, 4, 1, 0, 0), (5, 0, 5, 0, 0, 4)]]], [[[(1, 2, 1, 2, 0, 0), (2, 3, 2, 3, 0, 0)], [(1, 5, 1, 5, 0, 0), (0, 6, 0, 6, 0, 0)]], [[(1, 0, 1, 0, 0, 0), (4, 2, 4, 2, 0, 0)], [(3, 5, 3, 5, 0, 0), (6, 3, 6, 3, 0, 0)]]]]
K = max(len(ELEMENTS[0]), len(ELEMENTS[1]))
JC = 8
YC = 2 * JC
CHUNK = 128 * JC


def cas_matrix():
    counter = np.arange(64)
    angles = 2.0 * math.pi * (np.outer(counter, counter) % 64) / 64
    return np.cos(angles) + np.sin(angles)


def split_constant(matrix):
    high = matrix.astype(ml_dtypes.bfloat16)
    low = (matrix - high.astype(np.float64)).astype(ml_dtypes.bfloat16)
    return high, low


def lane_matrix():
    high, low = split_constant(np.kron(np.eye(2), cas_matrix()))
    row = np.concatenate([high, low], axis=1)
    return np.concatenate([row, row], axis=0)


def sublane_matrix():
    high, low = split_constant(cas_matrix())
    return np.concatenate([np.concatenate([high, high], 1), np.concatenate([low, low], 1)], 0)


def screened_table():
    counter = np.arange(64)
    wave = np.minimum(counter, 64 - counter) * (2.0 * math.pi / CELL_LENGTH)
    square = wave[:, None, None] ** 2 + wave[None, :, None] ** 2 + wave[None, None, :] ** 2
    guarded = np.where(square > 0.0, square, 1.0)
    screened = 4.0 * math.pi / guarded * -np.expm1(-guarded / (4.0 * SCREEN_OMEGA**2))
    table = np.where(square > 0.0, screened, 0.0) * (-1.0 / (NX * NY * NZ))
    return np.concatenate([table, table], axis=2).astype(np.float32)


def dot(a, b):
    return jnp.dot(a, b, preferred_element_type=F32)


def halves(v):
    high = v.astype(BF16)
    low = (v - high.astype(F32)).astype(BF16)
    return high, low


def along_lanes(v, weights):
    out = dot(jnp.concatenate(halves(v), axis=1), weights)
    return out[:, :128] + out[:, 128:]


def along_rows(v, weights):
    out = dot(weights, jnp.concatenate(halves(v), axis=0))
    return out[:64] + out[64:]


def rows_to_lanes(v, count):
    return jnp.concatenate([v[64 * i : 64 * i + 64] for i in range(count)], axis=1)


def lanes_to_rows(v, count):
    return jnp.concatenate([v[:, 128 * i : 128 * i + 128] for i in range(count)], axis=0)


class Place:
    def __init__(self):
        band = lax.axis_index("band")
        pair = lax.axis_index("pair")
        self.z, self.y, self.h = band // 8, (band // 2) % 4, band % 2
        self.l, self.c = pair // 2, pair % 2
        self.band = band

    def shifted(self, u, sign):
        z = (self.z + 4 + sign * u[0]) % 4
        y = (self.y + 4 + sign * u[1]) % 4
        h = (self.h + u[2]) % 2
        return z, y, h

    def band_at(self, u, sign):
        z, y, h = self.shifted(u, sign)
        return (z * 4 + y) * 2 + h

    def phase_at(self, mask, u, sign):
        z, y, h = self.shifted(u, sign)
        bits = (z // 2, y // 2, h)
        return sum(bit for k, bit in enumerate(bits) if mask >> k & 1) % 2


class Transfer:
    def __init__(self, place, l, e, step, from_l, slot, mask=0, value=0):
        self.l, self.e, self.step, self.from_l, self.slot = l, e, step, from_l, slot
        self.here, self.mine = place.l == from_l, place.l == l
        if mask:
            self.here = self.here & (place.phase_at(mask, step, -1) == value)
            self.mine = self.mine & (place.phase_at(mask, (0, 0, 0), 1) == value)


def transfers(place):
    found = []
    for l in (0, 1):
        for e, (first, second, mask, relay) in enumerate(ELEMENTS[l]):
            if relay is not None:
                found.append(Transfer(place, l, e, *relay))
                continue
            for value, u in enumerate((first, second) if mask else (first,)):
                from_l = l if u[2] == 0 else 1 - l
                found.append(Transfer(place, l, e, u, from_l, 0, mask, value))
    return found


def kernel(orb_ref, keep_ref, wz_ref, wr_ref, table_hbm, out_ref,
           slots, acc, xbuf, rbuf, fbuf, spect, table,
           local_sem, d_send, d_recv, f_send, f_recv, x_send, x_recv, r_send, r_recv, s_send, s_recv):
    at = Place()
    l, c = at.l, at.c
    sibling = (at.band, 2 * l + 1 - c)
    twin = (at.band, 2 * (1 - l) + c)

    def pick(values):
        out = 0
        for (pl_, pc_), value in values.items():
            if value != 0:
                out = out + value * ((l == pl_) & (c == pc_)).astype(jnp.int32)
        return out

    own_copy = pltpu.make_async_copy(orb_ref, slots.at[0], local_sem.at[0])
    own_copy.start()
    table_copy = pltpu.make_async_copy(table_hbm, table, local_sem.at[1])
    table_copy.start()

    barrier = pltpu.get_barrier_semaphore()
    peers = 2
    pl.semaphore_signal(barrier, inc=1, device_id=sibling, device_id_type=MESH)
    pl.semaphore_signal(barrier, inc=1, device_id=twin, device_id_type=MESH)
    moves = transfers(at)

    def child(move):
        return (at.band_at(move.step, -1), 2 * move.l + c)

    def parent(move):
        return (at.band_at(move.step, 1), 2 * move.from_l + c)

    for move in moves:
        peers = peers + move.here.astype(jnp.int32) + move.mine.astype(jnp.int32)

        @pl.when(move.here)
        def _():
            pl.semaphore_signal(barrier, inc=1, device_id=child(move), device_id_type=MESH)

        @pl.when(move.mine)
        def _():
            pl.semaphore_signal(barrier, inc=1, device_id=parent(move), device_id_type=MESH)

    own_copy.wait()
    pl.semaphore_wait(barrier, peers)

    my_rows = pl.ds(pl.multiple_of(32 * c, 32), 32)

    def chunk(i):
        return pl.ds(pl.multiple_of(i * CHUNK, CHUNK), CHUNK)

    everything = pl.ds(0, NYZ)

    def orbital_out(move, lanes, i=0):
        return pltpu.make_async_remote_copy(
            src_ref=slots.at[move.slot, my_rows, lanes],
            dst_ref=slots.at[move.e + 1, my_rows, lanes],
            send_sem=d_send.at[move.l * K + move.e], recv_sem=d_recv.at[move.e * 4 + i],
            device_id=child(move), device_id_type=MESH)

    def is_early(move):
        return move.e in EARLY_NEAR[move.l] or move.e in EARLY_FAR[move.l]

    def set_out(early, i):
        for move in moves:
            if move.slot == 0 and is_early(move) == early:

                @pl.when(move.here)
                def _():
                    orbital_out(move, chunk(i), i).start()

    for i in range(4):
        set_out(True, i)

    for e in range(1, K + 1):
        acc[e] = jnp.zeros(acc.shape[1:], F32)

    def forward(e, lanes, i=0):
        return pltpu.make_async_remote_copy(
            src_ref=slots.at[e + 1, my_rows, lanes], dst_ref=slots.at[e + 1, my_rows, lanes],
            send_sem=f_send.at[e], recv_sem=f_recv.at[e * 4 + i],
            device_id=sibling, device_id_type=MESH)

    def for_chip(chosen, body):
        for chip in (0, 1):
            if chosen[chip]:

                @pl.when(l == chip)
                def _():
                    for e in chosen[chip]:
                        body(chip, e)

    def pass_on(chosen, i):
        def relayed(chip, e):
            return any((move.from_l, move.slot) == (chip, e + 1) for move in moves)

        chosen = [sorted(chosen[chip], key=lambda e: not relayed(chip, e)) for chip in (0, 1)]

        def one(chip, e):
            arriving = [move for move in moves if (move.l, move.e) == (chip, e)][0]
            orbital_out(arriving, chunk(i), i).wait_recv()
            forward(e, chunk(i), i).start()
            for move in moves:
                if (move.from_l, move.slot) == (chip, e + 1):
                    orbital_out(move, chunk(i), i).start()

        for_chip(chosen, one)

    def passed_on(chosen, i):
        for_chip(chosen, lambda chip, e: forward(e, chunk(i), i).wait_recv())

    low_lanes = lax.broadcasted_iota(jnp.int32, (64, 128), 1) < 64

    def lanes_of(i):
        return chunk(i)

    def transform(pairs, update, before=None, middle=None, after=None):
        wz, wr = wz_ref[...], wr_ref[...]
        (p0, q0), (p1, q1) = pairs

        def first(i, carry):
            if before is not None:
                before(i)
            lanes = lanes_of(i)
            d0 = slots[p0, :, lanes] * slots[q0, :, lanes]
            d1 = slots[p1, :, lanes] * slots[q1, :, lanes]
            tiles = []
            for j in range(JC):
                t0, t1 = d0[:, 128 * j : 128 * j + 128], d1[:, 128 * j : 128 * j + 128]
                tiles.append(jnp.where(low_lanes, t0, pltpu.roll(t1, 64, 1)))
                tiles.append(jnp.where(low_lanes, pltpu.roll(t0, 64, 1), t1))
            v = along_lanes(jnp.concatenate(tiles, axis=0), wz)
            v = along_rows(rows_to_lanes(v, YC), wr)
            spect[pl.ds(pl.multiple_of(i * (64 * YC), 64 * YC), 64 * YC), :] = lanes_to_rows(v, YC)
            return carry

        def second(i, carry):
            if middle is not None:
                middle(i)
            rows = [pl.ds(i * YC + k, 64, stride=64) for k in range(YC)]
            v = along_rows(jnp.concatenate([spect[r, :] for r in rows], axis=1), wr)
            scale = jnp.concatenate([table[i * YC + k] for k in range(YC)], axis=1)
            v = along_rows(v * scale, wr)
            for k in range(YC):
                spect[rows[k], :] = v[:, 128 * k : 128 * k + 128]
            return carry

        def third(i, carry):
            v = spect[pl.ds(pl.multiple_of(i * (64 * YC), 64 * YC), 64 * YC), :]
            v = along_rows(rows_to_lanes(v, YC), wr)
            v = along_lanes(lanes_to_rows(v, YC), wz)
            v0, v1 = [], []
            for j in range(JC):
                even, odd = v[128 * j : 128 * j + 64], v[128 * j + 64 : 128 * j + 128]
                v0.append(jnp.where(low_lanes, even, pltpu.roll(odd, 64, 1)))
                v1.append(jnp.where(low_lanes, pltpu.roll(even, 64, 1), odd))
            update(lanes_of(i), jnp.concatenate(v0, axis=1), jnp.concatenate(v1, axis=1))
            if after is not None:
                after(i)
            return carry

        lax.fori_loop(0, 64 // YC, first, 0)
        lax.fori_loop(0, 64 // YC, second, 0, unroll=True)
        lax.fori_loop(0, 64 // YC, third, 0)

    def keep_at(i, j):
        return keep_ref[i, j].astype(F32)

    self_keep = keep_at(at.band, at.band)

    def self_update(lanes, v0, v1):
        orbital = slots[0, :, lanes]
        for s in range(4):
            rows = slice(16 * s, 16 * s + 16)
            mine = self_keep * (2 * l + c == s).astype(F32)
            acc[0, s % 2, s // 2, :, lanes] = (mine * v0[rows]) * orbital[rows]

    def pair_batch(b, before, middle, after):
        pairs, scales = [], []
        for k in range(2):
            entries = {(pl_, pc_): PAIRS[pl_][pc_][b][k] for pl_ in (0, 1) for pc_ in (0, 1)}

            def value(field):
                return pick({key: field(entry) for key, entry in entries.items()})

            bits = (at.z // 2, at.y // 2, at.h)
            phase = sum(value(lambda t: t[4] >> n & 1) * bits[n] for n in range(3)) % 2
            unused = sum(value(lambda t: t[5] >> n & 1) * bits[n] for n in range(3)) % 2

            def both(field):
                v0 = value(lambda t: field(t, 0))
                return v0 + phase * (value(lambda t: field(t, 1)) - v0)

            p = both(lambda t, w: t[2 * w])
            q = both(lambda t, w: t[2 * w + 1])

            def band_of(which):
                def part(axis):
                    def get(host_l, t, w):
                        index = t[2 * w + which]
                        if index == 0:
                            return 0
                        element = ELEMENTS[host_l][index - 1]
                        return element[1 if (element[2] and w == 1) else 0][axis]

                    def table_of(w):
                        return pick({key: get(key[0], entry, w) for key, entry in entries.items()})

                    v0 = table_of(0)
                    return v0 + phase * (table_of(1) - v0)

                z = (at.z + part(0)) % 4
                y = (at.y + part(1)) % 4
                h = (at.h + part(2)) % 2
                return (z * 4 + y) * 2 + h

            weight = keep_at(band_of(0), band_of(1))
            pairs.append((p, q))
            scales.append(weight * (jnp.int32(1) - unused).astype(F32))

        def update(lanes, v0, v1):
            for (p, q), scale, v in zip(pairs, scales, (v0, v1)):
                scaled = scale * v
                to_p = scaled * slots[q, :, lanes]
                to_q = scaled * slots[p, :, lanes]
                for target, term in ((p, to_p), (q, to_q)):
                    for s in range(4):
                        acc[target, s % 2, s // 2, :, lanes] += term[16 * s : 16 * s + 16]

        transform(pairs, update, before, middle, after)

    def exchange(e, lanes, i=0):
        return pltpu.make_async_remote_copy(
            src_ref=acc.at[e, 1 - c, :, :, lanes], dst_ref=xbuf.at[e, :, :, lanes],
            send_sem=x_send.at[e], recv_sem=x_recv.at[e * 4 + i],
            device_id=sibling, device_id_type=MESH)

    def send_back(move, lanes, i=0):
        return pltpu.make_async_remote_copy(
            src_ref=acc.at[move.e + 1, c, :, :, lanes],
            dst_ref=rbuf.at[move.l * K + move.e, :, :, lanes],
            send_sem=r_send.at[move.e], recv_sem=r_recv.at[(move.l * K + move.e) * 4 + i],
            device_id=parent(move), device_id_type=MESH)

    def swap(lanes, i=0):
        return pltpu.make_async_remote_copy(
            src_ref=acc.at[0, c, 1 - l, :, lanes], dst_ref=fbuf.at[:, lanes],
            send_sem=s_send.at[0], recv_sem=s_recv.at[i], device_id=twin, device_id_type=MESH)

    def start_return(chosen, i):
        for_chip(chosen, lambda chip, e: exchange(e + 1, chunk(i), i).start())

    def collect(move, e, lanes, i):
        send_back(move, lanes, i).wait_recv()
        acc[e, c, :, :, lanes] += rbuf[move.l * K + move.e, :, :, lanes]

    def finish_return(chosen, i):
        lanes = chunk(i)

        def one(chip, e):
            exchange(e + 1, lanes, i).wait_recv()
            acc[e + 1, c, :, :, lanes] += xbuf[e + 1, :, :, lanes]
            for move in moves:
                if (move.from_l, move.slot) == (chip, e + 1):
                    collect(move, e + 1, lanes, i)
            for move in moves:
                if (move.l, move.e) == (chip, e):

                    @pl.when(move.mine)
                    def _():
                        send_back(move, lanes, i).start()

        for_chip(chosen, one)

    def at_step(i, step, *actions):
        @pl.when(i == step)
        def _():
            for action, *arguments in actions:
                action(*arguments)

    def self_after(i):
        at_step(i, 3, (pass_on, EARLY_NEAR, 1))
        at_step(i, 3, *[(set_out, False, k) for k in range(4)])
        at_step(i, 0, (pass_on, EARLY_NEAR, 0))

    def first_before(i):
        for k in (1, 2, 3):
            at_step(i, k, (pass_on, EARLY_FAR, k))
        passed_on(EARLY_NEAR, i)
        passed_on(EARLY_FAR, i)

    def first_middle(i):
        at_step(i, 0, (pass_on, LATE_NEAR, 0))

    def first_after(i):
        start_return(BACK_EARLY, i)
        start_return(BACK_EARLY_JOIN, i)

        @pl.when(i > 1)
        def _():
            finish_return(BACK_EARLY, i - 2)

        @pl.when(i > 0)
        def _():
            pass_on(LATE_NEAR, i)

    def second_before(i):
        at_step(i, 1, (finish_return, BACK_EARLY, 3))
        pass_on(LATE_FAR, i)
        passed_on(LATE_NEAR, i)
        passed_on(LATE_FAR, i)

    def second_after(i):
        start_return(BACK_LATE, i)
        start_return(BACK_LATE_JOIN, i)
        exchange(0, chunk(i), i).start()
        finish_return(BACK_EARLY_JOIN, i)

        @pl.when(i > 0)
        def _():
            finish_return(BACK_LATE, i - 1)

    table_copy.wait()
    transform([(0, 0), (0, 0)], self_update, after=self_after)
    for i in range(2, 4):
        pass_on(EARLY_NEAR, i)
    pass_on(EARLY_FAR, 0)
    pair_batch(0, first_before, first_middle, first_after)
    finish_return(BACK_EARLY, 2)
    pair_batch(1, second_before, None, second_after)
    finish_return(BACK_LATE, 3)

    def gather(i, carry):
        lanes = chunk(i)
        finish_return(BACK_LATE_JOIN, i)
        exchange(0, lanes, i).wait_recv()
        acc[0, c, :, :, lanes] += xbuf[0, :, :, lanes]
        for move in moves:
            if move.slot == 0:

                @pl.when(move.here)
                def _():
                    collect(move, 0, lanes, i)

        swap(lanes, i).start()
        return carry

    def finish(i, carry):
        lanes = chunk(i)
        swap(lanes, i).wait_recv()
        out_ref[:, lanes] = acc[0, c, l, :, lanes] + fbuf[:, lanes]
        return carry

    lax.fori_loop(0, 4, gather, 0)
    lax.fori_loop(0, 4, finish, 0)

    swap(everything).wait_send()
    exchange(0, everything).wait_send()
    elements = [range(len(ELEMENTS[0])), range(len(ELEMENTS[1]))]
    for_chip(elements, lambda chip, e: forward(e, everything).wait_send())
    for_chip(elements, lambda chip, e: exchange(e + 1, everything).wait_send())
    for move in moves:

        @pl.when(move.here)
        def _():
            orbital_out(move, everything).wait_send()

        @pl.when(move.mine)
        def _():
            send_back(move, everything).wait_send()


def body(orbitals, pair_keep, wz, wr, table):
    dma = pltpu.SemaphoreType.DMA
    out = pl.pallas_call(
        kernel,
        name="exchange",
        out_shape=jax.ShapeDtypeStruct((16, NYZ), F32),
        in_specs=[
            pl.BlockSpec(memory_space=pl.ANY),
            pl.BlockSpec(memory_space=pltpu.SMEM),
            pl.BlockSpec(memory_space=pltpu.VMEM),
            pl.BlockSpec(memory_space=pltpu.VMEM),
            pl.BlockSpec(memory_space=pl.ANY),
        ],
        out_specs=pl.BlockSpec(memory_space=pltpu.VMEM),
        scratch_shapes=[
            pltpu.VMEM((K + 1, NX, NYZ), F32),
            pltpu.VMEM((K + 1, 2, 2, 16, NYZ), F32),
            pltpu.VMEM((K + 1, 2, 16, NYZ), F32),
            pltpu.VMEM((2 * K, 2, 16, NYZ), F32),
            pltpu.VMEM((16, NYZ), F32),
            pltpu.VMEM((64 * 64, 128), F32),
            pltpu.VMEM((64, 64, 128), F32),
            dma((2,)),
            dma((2 * K,)), dma((4 * K,)),
            dma((K,)), dma((4 * K,)),
            dma((K + 1,)), dma((4 * K + 4,)),
            dma((K,)), dma((8 * K,)),
            dma((1,)), dma((4,)),
        ],
        compiler_params=pltpu.CompilerParams(
            collective_id=0, has_side_effects=True, vmem_limit_bytes=56 << 20),
    )(orbitals.reshape(NX, NYZ), pair_keep, wz, wr, table)
    return out.reshape(1, 16, NYZ)


def solution(mesh):
    constants = (lane_matrix(), sublane_matrix(), screened_table())

    def call(orbitals, pair_keep):
        return body(orbitals, pair_keep, *[jnp.asarray(x) for x in constants])

    return jax.shard_map(
        call,
        mesh=mesh,
        in_specs=(P("band", None, None), P()),
        out_specs=P("band", "pair", None),
        check_vma=False,
    )
```
